128 devices in a mesh: dp: 16 (over z, x), tensor: 8 (over y, core).
Axes of the slice: x: 4, y: 4, z: 4, core: 2. Of those that a mesh axis runs over, the one named last changes fastest.
Arguments:
- queries: bfloat16 [1024, 32, 128], P('dp'), may hold values from -5 to 5
- new_keys: bfloat16 [1024, 2, 128], P('dp'), may hold values from -5 to 5
- new_values: bfloat16 [1024, 2, 128], P('dp'), may hold values from -5 to 5
- key_cache: bfloat16 [1024, 2, 256, 128], P('dp', None, 'tensor'), may hold values from -160 to 160
- value_cache: bfloat16 [1024, 2, 256, 128], P('dp', None, 'tensor'), may hold values from -5 to 5
- lengths: int32 [1024], P('dp'), may hold values from 2 to 256, as said below
- residual_in: bfloat16 [1024, 4096], P(('dp', 'tensor')), may hold values from -24 to 24
- query_gain: float32 [128], replicated, may hold values from 0.1 to 1.9
- key_gain: float32 [128], replicated, may hold values from 0.1 to 1.9
- out_proj: bfloat16 [4096, 4096], P('tensor'), may hold values from -0.09375 to 0.09375
- norm_gain: float32 [4096], replicated, may hold values from 0.1 to 1.9
- expert_ids: int32 [1024, 8], P(('dp', 'tensor')), may hold values from 0 to 127, all different within a row; in each aligned block of 8 rows (0 to 7, 8 to 15, ...) at most 3 rows name the same one
- gate_weights: float32 [1024, 8], P(('dp', 'tensor')), may hold values from 0.05 to 1
- expert_gate: bfloat16 [128, 4096, 768], P(('dp', 'tensor')), may hold values from -0.09375 to 0.09375
- expert_up: bfloat16 [128, 4096, 768], P(('dp', 'tensor')), may hold values from -0.09375 to 0.09375
- expert_down: bfloat16 [128, 768, 4096], P(('dp', 'tensor')), may hold values from -0.21875 to 0.21875
Outputs:
- mixed: bfloat16 [1024, 4096], P(('dp', 'tensor'))
The draws below stay inside these ranges and needn't reach their ends.
Inputs may be any that keep to these rules, and one draw needn't show every extreme that they name: `expert_ids`: rows are taken in aligned blocks of 8; within a block no expert is named by more than 3 rows, a bound that some block reaches. `lengths`: each group of 64 rows has a row with 256 positions in use.
All inputs are finite; a program needn't handle non-finite values.
Results may differ from the reference program's by a relative error of at most 0.013.
Values may be sent and summed in bfloat16 or wider, within the bound.
A program may use at most 128 MiB of HBM per device.

```python
import math
import jax
import jax.numpy as jnp
import numpy as np
from jax import lax

D = 4096
QH = 32
KVH = 2
HD = 128
FFW = 768
TOPK = 8
CAP = 3
TOK_DEV = 8
GROUP = 16
EXPERTS = 128
ROWS_DEV = 64
TOKENS = 1024
CACHE = 256


def query_base(key):
    return jnp.clip(jax.random.normal(key, (TOKENS, QH, HD), jnp.float32), -5.0, 5.0)


def draw_queries(key, part):
    base_values = query_base(key)
    return base_values.astype(jnp.bfloat16)


def draw_key_cache(key, part):
    key = jax.random.fold_in(key, 2)
    shape = (TOKENS, KVH, CACHE, HD)
    keys_drawn = jnp.clip(jax.random.normal(key, shape, jnp.float32), -5.0, 5.0)
    return keys_drawn.astype(jnp.bfloat16)


def draw_lengths(key, part):
    key = jax.random.fold_in(key, 3)
    key_one, key_two = jax.random.split(key)
    drawn = jax.random.randint(key_one, (TOKENS,), 2, CACHE + 1, jnp.int32)
    chosen = jax.random.randint(key_two, (TOKENS // ROWS_DEV,), 0, ROWS_DEV, jnp.int32)
    row_index = jnp.arange(TOKENS, dtype=jnp.int32)
    longest = row_index % ROWS_DEV == chosen[row_index // ROWS_DEV]
    return jnp.where(longest, CACHE, drawn).astype(jnp.int32)


def draw_residual_in(key, part):
    key = jax.random.fold_in(key, 4)
    key_one, key_two, key_three = jax.random.split(key, 3)
    row_scale = jnp.exp(jax.random.uniform(key_two, (TOKENS, 1), jnp.float32, math.log(0.2), math.log(2.0)))
    column_scale = jnp.exp(jax.random.uniform(key_three, (1, D), jnp.float32, math.log(0.3), math.log(3.0)))
    base_values = jnp.clip(jax.random.normal(key_one, (TOKENS, D), jnp.float32), -4.0, 4.0)
    return (base_values * row_scale * column_scale).astype(jnp.bfloat16)


def block_levels(own_key, shape, cuts, low, high):
    def one(dim, blocks):
        heights = jax.random.uniform(jax.random.fold_in(jax.random.fold_in(own_key, 6), dim), (blocks,), jnp.float32, low / len(cuts), high / len(cuts))
        return jnp.repeat(jnp.exp(heights), shape[dim] // blocks).reshape((-1,) + (1,) * (len(shape) - dim - 1))

    factor_of = one(*cuts[0])
    for cut in cuts[1:]:
        factor_of = factor_of * one(*cut)
    return factor_of


def shared_out(own_key, own, number, rows, amount, top, bound, lean):
    order = jax.random.permutation(own_key, amount)
    heavy_load, common = portions_of(amount, rows * top, bound, lean, True), portions_of(amount, rows * top, bound, lean, False)
    places = jnp.arange(amount)

    def named(sizes, rotation):
        used = int((sizes > 0).sum())
        fixed = max(1, used // 4)
        moved = fixed + (places - fixed + rotation * (used - fixed)) % max(1, amount - fixed)
        return jnp.zeros((amount,), jnp.int32).at[order[jnp.where(places < fixed, places, moved)]].set(jnp.asarray(sizes, jnp.int32))

    sizes = jnp.where(number % 4 == 0, named(heavy_load, number // 4), named(common, number - number // 4 - 1))
    mixed = jax.random.permutation(jax.random.fold_in(own, 3), amount)
    source_of, sink = mixed[0:amount // 2 * 2:2], mixed[1:amount // 2 * 2:2]
    room = jnp.minimum(sizes[source_of] - 1, bound - sizes[sink]) // 2
    room = jnp.where((source_of == order[0]) | (sink == order[0]) | (sizes[sink] == 0), 0, jnp.maximum(room, 0))
    moved = jax.random.randint(jax.random.fold_in(own, 4), (amount // 2,), 0, 1 << 20) % (room + 1)
    sizes = sizes.at[source_of].add(-moved).at[sink].add(moved)
    labels = jnp.searchsorted(jnp.cumsum(sizes), jnp.arange(rows * top), side="right").astype(jnp.int32)
    listing = labels.reshape(top, rows).T
    listing = listing[jax.random.permutation(jax.random.fold_in(own, 1), rows)]
    rotation = jax.random.randint(jax.random.fold_in(own, 2), (rows, 1), 0, top)
    return jnp.take_along_axis(listing, (jnp.arange(top)[None, :] + rotation) % top, axis=1)


def portions_of(amount, total, most, lean, full):
    portions = [(1 << 20) // math.isqrt(grade ** lean) + 1 for grade in range(1, amount + 1)]
    largest = most if full else min(most, max(-(-total // amount), total * portions[0] // sum(portions)))
    least = 1 if total - largest >= amount - 1 else 0
    given, surplus = [largest] + [least] * (amount - 1), total - largest - least * (amount - 1)
    while surplus > 0:
        candidates = [i for i in range(1, amount) if given[i] < largest] or [i for i in range(1, amount) if given[i] < most]
        whole, budget = sum([portions[i] for i in candidates]), surplus
        for i in candidates:
            extra = min(most - given[i], max(1, budget * portions[i] // whole), surplus)
            given[i] = given[i] + extra
            surplus = surplus - extra
    return np.array(given)


def bell_draw(key, extent, deviation, limit, pieces=(), kind=jnp.bfloat16):
    values = jax.random.normal(key, extent, jnp.float32) * deviation
    if len(pieces) > 0:
        values = block_levels(key, extent, pieces, -0.22, 0.18) * values
    return jnp.clip(values, min=-limit, max=limit).astype(kind)


def setup_inputs(seed: int = 0) -> dict:
    splits = jax.random.split(jax.random.key(seed), 17)
    queries = draw_queries(jax.random.fold_in(splits[16], 71), 0)
    new_keys = bell_draw(splits[1], (TOKENS, KVH, HD), 1.0, 5.0, ((0, 16),))
    new_values = bell_draw(splits[2], (TOKENS, KVH, HD), 1.0, 5.0, ((0, 16),))
    key_cache = draw_key_cache(jax.random.fold_in(splits[16], 71), 0)
    value_cache = bell_draw(splits[4], (TOKENS, KVH, CACHE, HD), 1.0, 5.0, ((0, 16), (2, 8)))
    lengths = draw_lengths(jax.random.fold_in(splits[16], 71), 0)
    residual_in = draw_residual_in(jax.random.fold_in(splits[16], 71), 0)
    query_gain = jnp.clip(1.0 + 0.18 * jax.random.normal(splits[7], (HD,), jnp.float32), 0.1, 1.9)
    key_gain = jnp.clip(1.0 + 0.18 * jax.random.normal(splits[8], (HD,), jnp.float32), 0.1, 1.9)
    out_proj = bell_draw(splits[9], (QH * HD, D), (QH * HD) ** -0.5, 0.09375, ((0, 8),))
    norm_gain = jnp.clip(1.0 + 0.18 * jax.random.normal(splits[10], (D,), jnp.float32), 0.1, 1.9)
    expert_ids_keys = jax.random.split(jax.random.fold_in(splits[11], 1), TOKENS // TOK_DEV)
    expert_ids_turns = jax.random.permutation(jax.random.fold_in(splits[11], 3), TOKENS // TOK_DEV)
    expert_ids = jax.vmap(lambda own, number: shared_out(jax.random.fold_in(splits[11], 2), own, number, TOK_DEV, EXPERTS, TOPK, CAP, 2))(expert_ids_keys, expert_ids_turns).reshape((TOKENS, TOPK))
    gate_weights = jnp.clip(jnp.exp(math.log(1.0) - 2.9957323 * jax.random.uniform(splits[12], (TOKENS, TOPK), jnp.float32) ** block_levels(splits[12], (TOKENS, TOPK), ((0, 128),), -0.2, 0.2)), 0.05, 1.0)
    expert_gate = bell_draw(splits[13], (EXPERTS, D, FFW), D ** -0.5, 0.09375, ((0, 128),))
    expert_up = bell_draw(splits[14], (EXPERTS, D, FFW), D ** -0.5, 0.09375, ((0, 128),))
    expert_down = bell_draw(splits[15], (EXPERTS, FFW, D), FFW ** -0.5, 0.21875, ((0, 128),))
    return {"queries": queries, "new_keys": new_keys, "new_values": new_values, "key_cache": key_cache, "value_cache": value_cache, "lengths": lengths, "residual_in": residual_in, "query_gain": query_gain, "key_gain": key_gain, "out_proj": out_proj, "norm_gain": norm_gain, "expert_ids": expert_ids, "gate_weights": gate_weights, "expert_gate": expert_gate, "expert_up": expert_up, "expert_down": expert_down}


def rms_scale(values, gain):
    mean_sq = lax.optimization_barrier(jnp.mean(values * values, axis=-1, keepdims=True))
    return values * lax.rsqrt(mean_sq + 1e-06) * gain

def reference(queries, new_keys, new_values, key_cache, value_cache, lengths, residual_in, query_gain, key_gain, out_proj, norm_gain, expert_ids, gate_weights, expert_gate, expert_up, expert_down):
    highest = lax.Precision.HIGHEST
    query_norm = rms_scale(queries.astype(jnp.float32), query_gain.astype(jnp.float32)).astype(jnp.bfloat16)
    key_norm = rms_scale(new_keys.astype(jnp.float32), key_gain.astype(jnp.float32)).astype(jnp.bfloat16)
    grouped = query_norm.astype(jnp.float32).reshape(TOKENS, KVH, GROUP, HD)
    scaling = HD ** (-0.5)
    cache_scores = jnp.einsum('tgqd,tgpd->tgqp', grouped, key_cache.astype(jnp.float32), precision=highest) * scaling
    new_score = jnp.einsum('tgqd,tgd->tgq', grouped, key_norm.astype(jnp.float32), precision=highest) * scaling
    positions = jnp.arange(CACHE, dtype=jnp.int32)
    included = (positions[None, :] < lengths[:, None])[:, None, None, :]
    score_top = jnp.maximum(lax.optimization_barrier(jnp.max(jnp.where(included, cache_scores, -1e+30), axis=-1)), new_score)
    cache_weights = jnp.where(included, jnp.exp(cache_scores - score_top[..., None]), 0.0).astype(jnp.bfloat16)
    new_weight = jnp.exp(new_score - score_top).astype(jnp.bfloat16)
    weight_sum = lax.optimization_barrier(jnp.sum(cache_weights.astype(jnp.float32), axis=-1)) + new_weight.astype(jnp.float32)
    numerator = jnp.einsum('tgqp,tgpd->tgqd', cache_weights.astype(jnp.float32), value_cache.astype(jnp.float32), precision=highest)
    numerator = numerator + new_weight.astype(jnp.float32)[..., None] * new_values.astype(jnp.float32)[:, :, None, :]
    attn_out = (numerator / weight_sum[..., None]).reshape(TOKENS, QH * HD).astype(jnp.bfloat16)
    projected = jnp.dot(attn_out, out_proj, preferred_element_type=jnp.float32)
    hidden = residual_in.astype(jnp.float32) + projected
    normed = rms_scale(hidden, norm_gain.astype(jnp.float32)).astype(jnp.bfloat16)
    assign_total = TOKENS * TOPK
    flat_ids = expert_ids.reshape(-1).astype(jnp.int32)
    token_of = jnp.arange(assign_total, dtype=jnp.int32) // TOPK
    sort_order = jnp.argsort(flat_ids, stable=True).astype(jnp.int32)
    counts = jnp.zeros((EXPERTS,), jnp.int32).at[flat_ids].add(1)
    offsets = jnp.cumsum(counts).astype(jnp.int32) - counts
    block_rows = 64
    block_count = (counts + block_rows - 1) // block_rows
    block_start = jnp.cumsum(block_count).astype(jnp.int32) - block_count
    block_total = (assign_total + block_rows - 1) // block_rows + EXPERTS

    def expert_block(index):
        owner_id = jnp.minimum(jnp.sum((block_start + block_count <= index).astype(jnp.int32)), EXPERTS - 1)
        local_block = index - block_start[owner_id]
        first_slot = offsets[owner_id] + local_block * block_rows
        slot_pos = first_slot + jnp.arange(block_rows, dtype=jnp.int32)
        is_live = (local_block < block_count[owner_id]) & (slot_pos < offsets[owner_id] + counts[owner_id])
        safe_pos = jnp.minimum(slot_pos, assign_total - 1)
        picked = normed[token_of[sort_order[safe_pos]]].astype(jnp.float32)
        gate_val = jnp.dot(picked, expert_gate[owner_id].astype(jnp.float32), precision=highest)
        up_val = jnp.dot(picked, expert_up[owner_id].astype(jnp.float32), precision=highest)
        activation = (jax.nn.silu(gate_val) * up_val).astype(jnp.bfloat16)
        result = jnp.dot(activation.astype(jnp.float32), expert_down[owner_id].astype(jnp.float32), precision=highest).astype(jnp.bfloat16)
        result = jnp.where(is_live[:, None], result, jnp.zeros((), jnp.bfloat16))
        return (result, jnp.where(is_live, slot_pos, assign_total).astype(jnp.int32))
    outputs, destinations = lax.map(expert_block, jnp.arange(block_total, dtype=jnp.int32))
    sorted_out = jnp.zeros((assign_total + 1, D), jnp.bfloat16).at[destinations.reshape(-1)].set(outputs.reshape(-1, D))
    assigned = jnp.zeros((assign_total, D), jnp.bfloat16).at[sort_order].set(sorted_out[:assign_total])
    route_weights = (gate_weights / lax.optimization_barrier(jnp.sum(gate_weights, axis=1, keepdims=True))).astype(jnp.bfloat16)
    moe_sum = lax.optimization_barrier(jnp.sum(route_weights.astype(jnp.float32)[:, :, None] * assigned.astype(jnp.float32).reshape(TOKENS, TOPK, D), axis=1))
    return (hidden + moe_sum).astype(jnp.bfloat16)
```

```python
import jax
import jax.numpy as jnp
from jax import lax
from jax.experimental import pallas as pl
from jax.experimental.pallas import tpu as pltpu
from jax.sharding import PartitionSpec as P

MESH = pl.DeviceIdType.MESH
F32 = jnp.float32
BF16 = jnp.bfloat16
VMEM = pltpu.VMEM

D = 4096
HALF = 2048
FFW = 768
SLOTS = 96
EPS = 1e-6
LOW = -1e30
OFFSET = (0, 640, 1280)
WIDTH = (640, 640, 768)
ORDER = (("x", "y", "z"), ("y", "z", "x"), ("z", "x", "y"))
PARTS = (0, 1, 2)


def iota(shape, dim):
    return lax.broadcasted_iota(jnp.int32, shape, dim)


def dot(a, b):
    return jnp.dot(a, b, preferred_element_type=F32)


def kernel(
    q_ref, nk_ref, nv_ref, kc_ref, vc_ref, len_ref, res_ref, qg_ref, kg_ref, ng_ref, ids_ref, gw_ref,
    wp_hbm, wg_hbm, wu_hbm, wd_hbm,
    out_ref,
    wp, wg, wu, wd,
    num_f, num_b, stat, stat_t, coef, rec_num, rec_stat, attn,
    send_b, rec_b, hidden, sq_own, sq_rec,
    meta, plane_meta,
    g0, g1, g2, disp, comb,
    xs0, xs1, xs2, xr0, xr1, xr2, x_full, perm, perm_t, act, act_p,
    ys0, ys1, ys2, yr0, yr1, yr2,
    ps0, ps1, ps2, rb0, rb1, rb2, ra_s0, ra_s1, ra_s2, ra_r0, ra_r1, ra_r2,
    fin_s, fin_r,
    w_sem, loc_sem, send_sem, recv_sem,
):
    g, xs, xr, ys, yr = (g0, g1, g2), (xs0, xs1, xs2), (xr0, xr1, xr2), (ys0, ys1, ys2), (yr0, yr1, yr2)
    ps, rb, ra_s, ra_r = (ps0, ps1, ps2), (rb0, rb1, rb2), (ra_s0, ra_s1, ra_s2), (ra_r0, ra_r1, ra_r2)
    dp = lax.axis_index("dp")
    t = lax.axis_index("tensor")
    here = {"z": dp // 4, "x": dp % 4, "y": t // 2, "c": t % 2}
    c = here["c"]

    def device(**moved):
        at = dict(here, **moved)
        return (at["z"] * 4 + at["x"], at["y"] * 2 + at["c"])

    def along(axis, k):
        return (here[axis] + k) % 4

    def tensor_peer(k):
        return (dp, (t + k) % 8)

    counter = [0]
    sent = []

    def remote(src, dst, to):
        i = counter[0]
        counter[0] += 1
        copy = pltpu.make_async_remote_copy(
            src_ref=src,
            dst_ref=dst,
            send_sem=send_sem.at[i],
            recv_sem=recv_sem.at[i],
            device_id=to,
            device_id_type=MESH,
        )
        copy.start()
        sent.append(copy)
        return copy

    sibling = device(c=1 - c)

    weights = []
    for i, (src, dst) in enumerate(
        ((wp_hbm, wp), (wg_hbm.at[0], wg), (wu_hbm.at[0], wu), (wd_hbm.at[0], wd))
    ):
        weights.append(pltpu.make_async_copy(src, dst, w_sem.at[i]))
        weights[-1].start()

    barrier = pltpu.get_barrier_semaphore()
    peers = [tensor_peer(k) for k in range(1, 8)]
    for axis in ("x", "z"):
        for k in (1, 2, 3):
            for core in (0, 1):
                peers.append(device(**{axis: along(axis, k), "c": core}))
    for peer in peers:
        pl.semaphore_signal(barrier, inc=1, device_id=peer, device_id_type=MESH)
    pl.semaphore_wait(barrier, len(peers))

    own_rows = pl.ds(pl.multiple_of(c * 8, 8), 8)
    other_rows = pl.ds(pl.multiple_of((1 - c) * 8, 8), 8)
    own_cols = pl.ds(pl.multiple_of(c * HALF, HALF), HALF)
    other_cols = pl.ds(pl.multiple_of((1 - c) * HALF, HALF), HALF)
    hidden[own_rows, :] = res_ref[:, own_cols].astype(F32)
    fin_s[0] = res_ref[:, other_cols].astype(F32)
    res_copy = remote(fin_s.at[0], hidden.at[own_rows, :], sibling)

    gw = gw_ref[...]
    route = (gw / jnp.sum(gw, axis=1, keepdims=True)).astype(BF16)
    put = iota((8, 128), 1) - iota((8, 128), 0)
    ids = ids_ref[...].astype(F32).astype(BF16)
    table = dot(ids, (put == 0).astype(F32).astype(BF16)) + dot(
        route, (put == 8).astype(F32).astype(BF16)
    )
    z, x, y = here["z"], here["x"], here["y"]
    meta[z, x, y, c] = table
    spread = [
        remote(meta.at[z, x, y, c], meta.at[z, x, y, c], tensor_peer(k)) for k in range(1, 8)
    ]

    scaling = 128.0**-0.5
    first = (t == 0).astype(F32)
    shuffle = (iota((128, 128), 1) == (iota((128, 128), 0) % 8) * 16 + iota((128, 128), 0) // 8)
    shuffle = shuffle.astype(F32).astype(BF16)
    lane_row = iota((1, 256), 1) // 32
    lane_pos = iota((1, 256), 1) % 32 + t * 32
    own_block = (iota((128, 256), 0) % 8) == (iota((128, 256), 1) // 32)
    ones = jnp.ones((256, 128), BF16)
    lane = iota((8, 128), 1)
    stat[...] = jnp.zeros_like(stat)

    def attend(blk, carry):
        at = pl.multiple_of(blk * 8, 8)
        rows = pl.ds(at, 8)
        limit = jnp.zeros((1, 256), jnp.int32)
        for r in range(8):
            limit = jnp.where(lane_row == r, len_ref[at + r], limit)
        bias = jnp.where(lane_pos < limit, 0.0, LOW)
        stats = jnp.zeros((8, 128), F32)
        for kv in range(2):
            q = q_ref[rows, pl.ds(kv * 16, 16), :].astype(F32).reshape(128, 128)
            q = q * lax.rsqrt(jnp.mean(q * q, axis=1, keepdims=True) + EPS) * qg_ref[...]
            q = dot(shuffle, q.astype(BF16)).astype(BF16)
            nk = nk_ref[rows, kv, :].astype(F32)
            nk = nk * lax.rsqrt(jnp.mean(nk * nk, axis=1, keepdims=True) + EPS) * kg_ref[...]
            nk = nk.astype(BF16).astype(F32)
            nv = nv_ref[rows, kv, :].astype(F32)
            keys = kc_ref[rows, kv].reshape(256, 128)
            values = vc_ref[rows, kv].reshape(256, 128)
            score = lax.dot_general(
                q, keys, (((1,), (1,)), ((), ())), preferred_element_type=F32
            )
            score = jnp.where(own_block, score * scaling + bias, LOW)
            fresh = (q.astype(F32).reshape(16, 8, 128) * nk[None]).reshape(128, 128)
            fresh = jnp.sum(fresh, axis=1, keepdims=True) * scaling
            top = jnp.maximum(jnp.max(score, axis=1, keepdims=True), fresh)
            weight = jnp.exp(score - top).astype(BF16)
            new_weight = jnp.exp(fresh - top).astype(BF16).astype(F32) * first
            number = dot(weight, values)
            total = dot(weight, ones) + new_weight
            number = number.reshape(16, 8, 128) + new_weight.reshape(16, 8, 1) * nv[None]
            top = jnp.broadcast_to(top, (128, 128)).reshape(16, 8, 128)
            total = total.reshape(16, 8, 128)
            for i in range(16):
                head = kv * 16 + i
                num_f[head, rows, :] = number[i]
                column = 8 * (head // 4) + head % 4
                stats = jnp.where(lane == column, top[i], stats)
                stats = jnp.where(lane == column + 4, total[i], stats)
        stat[rows, :] = stats
        return carry

    lax.fori_loop(0, 8, attend, 0)
    stat_t[...] = stat[...].T
    num_b[...] = num_f[...].astype(BF16)
    partials = []
    for k in (4, 3, 5, 2, 6, 1, 7):
        to = (t + k) % 8
        tile = pl.ds(pl.multiple_of(to * 8, 8), 8)
        partials.append(remote(stat_t.at[tile, :], rec_stat.at[k], (dp, to)))
        partials.append(remote(num_b.at[pl.ds(to * 4, 4)], rec_num.at[k], (dp, to)))

    for copy in spread:
        copy.wait_recv()
    spread = [
        remote(meta.at[z, x], meta.at[z, x], device(x=along("x", k))) for k in (1, 2, 3)
    ]
    rec_num[0] = num_b[pl.ds(t * 4, 4)]
    rec_stat[0] = stat_t[pl.ds(pl.multiple_of(t * 8, 8), 8), :]
    row = iota((384, 384), 0)
    col = iota((384, 384), 1)
    zz, yy, xx, rest = row // 96, (row // 24) % 4, (row // 6) % 4, row % 6
    perm[0] = (col == xx * 96 + zz * 24 + yy * 6 + rest).astype(F32).astype(BF16)
    perm[1] = (col == yy * 96 + xx * 24 + zz * 6 + rest).astype(F32).astype(BF16)
    zz, yy, xx, rest = col // 96, (col // 24) % 4, (col // 6) % 4, col % 6
    perm_t[0] = (row == xx * 96 + zz * 24 + yy * 6 + rest).astype(F32).astype(BF16)
    perm_t[1] = (row == yy * 96 + xx * 24 + zz * 6 + rest).astype(F32).astype(BF16)

    for copy in partials:
        copy.wait_recv()
    tops = [rec_stat[k][0:4] for k in range(8)]
    best = tops[0]
    for top in tops[1:]:
        best = jnp.maximum(best, top)
    scale = [jnp.exp(top - best) for top in tops]
    whole = scale[0] * rec_stat[0][4:8]
    for k in range(1, 8):
        whole = whole + scale[k] * rec_stat[k][4:8]
    coef[...] = jnp.zeros_like(coef)
    for k in range(8):
        coef[8 * k : 8 * k + 4, :] = scale[k] / whole
    columns = coef[...].T
    for j in range(4):
        out = jnp.zeros((64, 128), F32)
        for k in range(8):
            out = out + columns[0:64, 8 * k + j : 8 * k + j + 1] * rec_num[k, j].astype(F32)
        attn[:, 128 * j : 128 * j + 128] = out.astype(BF16)

    for copy in spread:
        copy.wait_recv()
    spread = [remote(meta.at[z], meta.at[z], device(z=along("z", k))) for k in (1, 2, 3)]

    weights[0].wait()
    for half in (0, 1):
        for tile in range(0, HALF, 512):
            send_b[half, :, tile : tile + 512] = dot(
                attn[...], wp[:, half * HALF + tile : half * HALF + tile + 512]
            ).astype(BF16)
    shares = []
    for k in (4, 3, 5, 2, 6, 1, 7):
        to = (t + k) % 8
        rows = pl.ds(pl.multiple_of((to // 2) * 16, 16), 16)
        shares.append(remote(send_b.at[to % 2, rows, :], rec_b.at[k], (dp, to)))

    for copy in spread:
        copy.wait_recv()
    before = iota((256, 256), 0)
    after = iota((256, 256), 1)
    earlier = ((before // 8 == after // 8) & (before < after)).astype(F32).astype(BF16)
    slot_base = ((iota((1, 256), 1) // 8) * 3).astype(F32)
    slot_id = iota((SLOTS, 256), 0).astype(F32)
    for p in PARTS:
        a, b, last = ORDER[p]
        for ib in range(4):
            for ia in range(4):
                at = dict(here, **{a: ia, b: ib})
                plane_meta[pl.ds((ib * 4 + ia) * 16, 16), :] = meta[
                    at["z"], at["x"], at["y"]
                ].reshape(16, 128)
        table = plane_meta[...].T
        chosen, gates = table[0:8], table[8:16]
        for k in range(4):
            for core in range(2):
                at = dict(here, **{last: k, "c": core})
                expert = (at["z"] * 32 + at["x"] * 8 + at["y"] * 2 + at["c"]).astype(F32)
                hit = (chosen == expert).astype(F32)
                used = jnp.sum(hit, axis=0, keepdims=True)
                gate = jnp.sum(hit * gates, axis=0, keepdims=True)
                rank = dot(jnp.broadcast_to(used, (8, 256)).astype(BF16), earlier)[0:1]
                slot = jnp.where(used > 0.5, slot_base + rank, -1.0)
                match = slot == slot_id
                first_slot = (k * 2 + core) * SLOTS
                disp[p, first_slot : first_slot + SLOTS, :] = match.astype(F32).astype(BF16)
                comb[p, first_slot : first_slot + SLOTS, :] = jnp.where(match, gate, 0.0).astype(BF16)

    res_copy.wait_recv()
    for copy in shares:
        copy.wait_recv()
    rows = pl.ds(pl.multiple_of(y * 16, 16), 16)
    total = send_b[c, rows, :].astype(F32)
    for k in range(1, 8):
        total = total + rec_b[k].astype(F32)
    value = hidden[...] + total
    hidden[...] = value
    squares = jnp.sum(value * value, axis=1, keepdims=True)
    sq_own[...] = jnp.broadcast_to(squares, (16, 128))
    sq_copy = remote(sq_own, sq_rec, sibling)
    sq_copy.wait_recv()
    mean = (squares + sq_rec[:, 0:1]) * (1.0 / D)
    normed = (value * lax.rsqrt(mean + EPS) * ng_ref[pl.ds(c, 1), :]).astype(BF16)

    stage = []
    for p in PARTS:
        a, b, last = ORDER[p]
        g[p][here[b], here[a]] = normed[:, OFFSET[p] : OFFSET[p] + WIDTH[p]]
        unit = g[p].at[here[b], here[a]]
        stage.append([remote(unit, unit, device(**{a: along(a, k)})) for k in (2, 1, 3)])
    for p in PARTS:
        a, b, last = ORDER[p]
        for copy in stage[p]:
            copy.wait_recv()
        unit = g[p].at[here[b]]
        stage[p] = [remote(unit, unit, device(**{b: along(b, k)})) for k in (2, 1, 3)]
    arriving, locals_in = [], []
    for p in PARTS:
        a, b, last = ORDER[p]
        for copy in stage[p]:
            copy.wait_recv()
        plane = g[p][...].reshape(256, WIDTH[p])
        copies = []
        for k in (2, 1, 3, 0):
            to = along(last, k)
            wanted = disp[p, pl.ds(pl.multiple_of(to * 2 * SLOTS, 2 * SLOTS), 2 * SLOTS), :]
            xs[p][k] = dot(wanted, plane).astype(BF16).reshape(2, SLOTS, WIDTH[p])
            for j in (0, 1):
                core = (c + j) % 2
                src = xs[p].at[k, core]
                dst = xr[p].at[c, here[last]]
                if k == 0 and j == 0:
                    local = pltpu.make_async_copy(src, dst, loc_sem.at[p])
                    local.start()
                    locals_in.append(local)
                else:
                    copies.append(remote(src, dst, device(**{last: to, "c": core})))
        arriving.append(copies)
    for p in PARTS:
        for copy in arriving[p]:
            copy.wait_recv()
        locals_in[p].wait()
        for half in (0, 1):
            cols = slice(half * HALF + OFFSET[p], half * HALF + OFFSET[p] + WIDTH[p])
            block = xr[p][half].reshape(384, WIDTH[p])
            if p > 0:
                block = dot(perm[p - 1], block).astype(BF16)
            x_full[:, cols] = block

    for copy in weights[1:]:
        copy.wait()

    def expert(n, carry):
        cols = pl.ds(pl.multiple_of(n * 256, 256), 256)
        gate = dot(x_full[...], wg[:, cols])
        up = dot(x_full[...], wu[:, cols])
        act[:, cols] = (gate / (1.0 + jnp.exp(-gate)) * up).astype(BF16)
        return carry

    lax.fori_loop(0, FFW // 256, expert, 0)

    arriving, locals_out = [], []
    for p in PARTS:
        a, b, last = ORDER[p]
        if p == 0:
            act_p[...] = act[...]
        else:
            act_p[...] = dot(perm_t[p - 1], act[...]).astype(BF16)
        for half in (0, 1):
            cols = slice(half * HALF + OFFSET[p], half * HALF + OFFSET[p] + WIDTH[p])
            ys[p][half] = dot(act_p[...], wd[:, cols]).astype(BF16).reshape(4, SLOTS, WIDTH[p])
        copies = []
        for k in (2, 1, 3, 0):
            to = along(last, k)
            for j in (0, 1):
                core = (c + j) % 2
                src = ys[p].at[core, to]
                dst = yr[p].at[here[last] * 2 + c]
                if k == 0 and j == 0:
                    local = pltpu.make_async_copy(src, dst, loc_sem.at[3 + p])
                    local.start()
                    locals_out.append(local)
                else:
                    copies.append(remote(src, dst, device(**{last: to, "c": core})))
        arriving.append(copies)
    stage = []
    for p in PARTS:
        a, b, last = ORDER[p]
        for copy in arriving[p]:
            copy.wait_recv()
        locals_out[p].wait()
        summed = lax.dot_general(
            comb[p], yr[p][...].reshape(8 * SLOTS, WIDTH[p]), (((0,), (0,)), ((), ())),
            preferred_element_type=F32,
        )
        ps[p][...] = summed.astype(BF16).reshape(4, 64, WIDTH[p])
        copies = []
        for k in (2, 1, 3):
            to = along(b, k)
            copies.append(remote(ps[p].at[to], rb[p].at[k], device(**{b: to})))
        stage.append(copies)
    for p in PARTS:
        a, b, last = ORDER[p]
        for copy in stage[p]:
            copy.wait_recv()
        total = ps[p][here[b]].astype(F32)
        for k in (1, 2, 3):
            total = total + rb[p][k].astype(F32)
        ra_s[p][...] = total.astype(BF16).reshape(4, 16, WIDTH[p])
        copies = []
        for k in (2, 1, 3):
            to = along(a, k)
            copies.append(remote(ra_s[p].at[to], ra_r[p].at[k], device(**{a: to})))
        stage[p] = copies
    for p in PARTS:
        a, b, last = ORDER[p]
        for copy in stage[p]:
            copy.wait_recv()
        total = ra_s[p][here[a]].astype(F32)
        for k in (1, 2, 3):
            total = total + ra_r[p][k].astype(F32)
        cols = slice(OFFSET[p], OFFSET[p] + WIDTH[p])
        hidden[:, cols] = hidden[:, cols] + total

    fin_s[1] = hidden[other_rows, :]
    fin = remote(fin_s.at[1], fin_r, sibling)
    out_ref[:, own_cols] = hidden[own_rows, :].astype(BF16)
    fin.wait_recv()
    out_ref[:, other_cols] = fin_r[...].astype(BF16)
    for copy in sent:
        copy.wait_send()


COPIES = 7 + 3 + 3 + 1 + 14 + 7 + 1 + 9 + 9 + 21 + 21 + 9 + 9 + 1


def shards(
    queries, new_keys, new_values, key_cache, value_cache, lengths, residual_in, query_gain, key_gain,
    out_proj, norm_gain, expert_ids, gate_weights, expert_gate, expert_up, expert_down,
):
    vmem = pl.BlockSpec(memory_space=pltpu.VMEM)
    anywhere = pl.BlockSpec(memory_space=pl.ANY)

    def each(shape_of, dtype=BF16):
        return [VMEM(shape_of(w), dtype) for w in WIDTH]

    return pl.pallas_call(
        kernel,
        out_shape=jax.ShapeDtypeStruct((8, D), BF16),
        in_specs=[vmem] * 5 + [pl.BlockSpec(memory_space=pltpu.SMEM)] + [vmem] * 6 + [anywhere] * 4,
        out_specs=vmem,
        scratch_shapes=[
            VMEM((512, D), BF16), VMEM((D, FFW), BF16), VMEM((D, FFW), BF16), VMEM((FFW, D), BF16),
            VMEM((32, 64, 128), F32), VMEM((32, 64, 128), BF16), VMEM((128, 128), F32),
            VMEM((128, 128), F32), VMEM((128, 128), F32), VMEM((8, 4, 64, 128), BF16),
            VMEM((8, 8, 128), F32), VMEM((64, 512), BF16),
            VMEM((2, 64, HALF), BF16), VMEM((8, 16, HALF), BF16), VMEM((16, HALF), F32),
            VMEM((16, 128), F32), VMEM((16, 128), F32),
            VMEM((4, 4, 4, 2, 8, 128), F32), VMEM((256, 128), F32),
            *each(lambda w: (4, 4, 16, w)),
            VMEM((3, 8 * SLOTS, 256), BF16), VMEM((3, 8 * SLOTS, 256), BF16),
            *each(lambda w: (4, 2, SLOTS, w)),
            *each(lambda w: (2, 4, SLOTS, w)),
            VMEM((384, D), BF16), VMEM((2, 384, 384), BF16), VMEM((2, 384, 384), BF16),
            VMEM((384, FFW), BF16), VMEM((384, FFW), BF16),
            *each(lambda w: (2, 4, SLOTS, w)),
            *each(lambda w: (8, SLOTS, w)),
            *each(lambda w: (4, 64, w)), *each(lambda w: (4, 64, w)),
            *each(lambda w: (4, 16, w)), *each(lambda w: (4, 16, w)),
            VMEM((2, 8, HALF), F32), VMEM((8, HALF), F32),
            pltpu.SemaphoreType.DMA((4,)), pltpu.SemaphoreType.DMA((6,)),
            pltpu.SemaphoreType.DMA((COPIES,)), pltpu.SemaphoreType.DMA((COPIES,)),
        ],
        compiler_params=pltpu.CompilerParams(
            collective_id=0, has_side_effects=True, vmem_limit_bytes=60 * 2**20
        ),
        cost_estimate=pl.CostEstimate(flops=10**10, bytes_accessed=26 * 2**20, transcendentals=10**6),
    )(
        queries, new_keys, new_values, key_cache, value_cache, lengths, residual_in,
        query_gain.reshape(1, 128), key_gain.reshape(1, 128), norm_gain.reshape(2, HALF),
        expert_ids, gate_weights, out_proj, expert_gate, expert_up, expert_down,
    )


def solution(mesh):
    rows = P(("dp", "tensor"), None)
    experts = P(("dp", "tensor"), None, None)
    cache = P("dp", None, "tensor", None)
    heads = P("dp", None, None)
    return jax.shard_map(
        shards,
        mesh=mesh,
        in_specs=(
            heads, heads, heads, cache, cache, P("dp"), rows, P(), P(),
            P("tensor", None), P(), rows, rows, experts, experts, experts,
        ),
        out_specs=rows,
        check_vma=False,
    )
```

```python
import jax
import jax.numpy as jnp
from jax import lax
from jax.experimental import pallas as pl
from jax.experimental.pallas import tpu as pltpu
from jax.sharding import PartitionSpec as P

MESH = pl.DeviceIdType.MESH
F32 = jnp.float32
BF16 = jnp.bfloat16
VMEM = pltpu.VMEM

D = 4096
HALF = 2048
FFW = 768
SLOTS = 96
EPS = 1e-6
LOW = -1e30
ORDER = (("x", "y", "z"), ("y", "z", "x"), ("z", "x", "y"))
WAVES = (((2, 0, 384), (0, 384, 256), (1, 640, 384)), ((2, 1024, 384), (0, 1408, 384), (1, 1792, 256)))
PARTS = tuple(part for wave in WAVES for part in wave)
FORTH = ((0, 1, 2), (3, 4, 5))
BACK = ((3, 4, 5), (0, 1, 2))


def iota(shape, dim):
    return lax.broadcasted_iota(jnp.int32, shape, dim)


def dot(a, b):
    return jnp.dot(a, b, preferred_element_type=F32)


def kernel(
    q_ref, nk_ref, nv_ref, kc_ref, vc_ref, len_ref, res_ref, qg_ref, kg_ref, ng_ref, ids_ref, gw_ref,
    wp_hbm, wg_hbm, wu_hbm, wd_hbm,
    out_ref,
    wp, wg, wu, wd,
    num_f, num_b, stat, stat_t, coef, rec_num, rec_stat, attn,
    pair_s, pair_r, send_b, rec_b, hidden, sq_own, sq_rec,
    table_s, table_r, packed, meta, plane_meta, disp, comb,
    x_full, perm, perm_t, acc, act, act_p,
    g, xs, xr, ys, yr, ps, rb, ra_s, ra_r,
    fin_s, fin_r,
    w_sem, loc_sem, send_sem, recv_sem,
):
    dp = lax.axis_index("dp")
    t = lax.axis_index("tensor")
    here = {"z": dp // 4, "x": dp % 4, "y": t // 2, "c": t % 2}
    c = here["c"]

    def device(**moved):
        at = dict(here, **moved)
        return (at["z"] * 4 + at["x"], at["y"] * 2 + at["c"])

    def along(axis, k):
        return (here[axis] + k) % 4

    def tensor_peer(k):
        return (dp, (t + k) % 8)

    counter = [0]
    sent = []

    def remote(src, dst, to, at=None, start=True):
        i = counter[0] if at is None else at
        counter[0] += at is None
        copy = pltpu.make_async_remote_copy(
            src_ref=src,
            dst_ref=dst,
            send_sem=send_sem.at[i],
            recv_sem=recv_sem.at[i],
            device_id=to,
            device_id_type=MESH,
        )
        if start:
            copy.start()
        if at is None or not start:
            sent.append(copy)
        return copy

    sibling = device(c=1 - c)

    weights = []
    for i, (src, dst) in enumerate(
        ((wp_hbm, wp), (wg_hbm.at[0], wg), (wu_hbm.at[0], wu), (wd_hbm.at[0], wd))
    ):
        weights.append(pltpu.make_async_copy(src, dst, w_sem.at[i]))
        weights[-1].start()

    barrier = pltpu.get_barrier_semaphore()
    peers = [tensor_peer(k) for k in range(1, 8)]
    for axis in ("x", "z"):
        for k in (1, 2, 3):
            for core in (0, 1):
                peers.append(device(**{axis: along(axis, k), "c": core}))
    for peer in peers:
        pl.semaphore_signal(barrier, inc=1, device_id=peer, device_id_type=MESH)
    pl.semaphore_wait(barrier, len(peers))

    own_rows = pl.ds(pl.multiple_of(c * 8, 8), 8)
    other_rows = pl.ds(pl.multiple_of((1 - c) * 8, 8), 8)
    own_cols = pl.ds(pl.multiple_of(c * HALF, HALF), HALF)
    other_cols = pl.ds(pl.multiple_of((1 - c) * HALF, HALF), HALF)
    hidden[own_rows, :] = res_ref[:, own_cols].astype(F32)
    fin_s[0] = res_ref[:, other_cols].astype(F32)
    res_copy = remote(fin_s.at[0], hidden.at[own_rows, :], sibling)

    gw = gw_ref[...]
    route = (gw / jnp.sum(gw, axis=1, keepdims=True)).astype(BF16)
    put = iota((8, 128), 1) - iota((8, 128), 0) - t * 16
    ids = ids_ref[...].astype(F32).astype(BF16)
    table = dot(ids, (put == 0).astype(F32).astype(BF16)) + dot(
        route, (put == 8).astype(F32).astype(BF16)
    )
    z, x, y = here["z"], here["x"], here["y"]
    table_s[...] = table
    spread = [remote(table_s, table_r.at[k], tensor_peer(k)) for k in range(1, 8)]

    scaling = 128.0**-0.5
    first = (t == 0).astype(F32)
    shuffle = (iota((128, 128), 1) == (iota((128, 128), 0) % 8) * 16 + iota((128, 128), 0) // 8)
    shuffle = shuffle.astype(F32).astype(BF16)
    lane_row = iota((1, 256), 1) // 32
    lane_pos = iota((1, 256), 1) % 32 + t * 32
    own_block = (iota((128, 256), 0) % 8) == (iota((128, 256), 1) // 32)
    ones = jnp.ones((256, 128), BF16)
    lane = iota((8, 128), 1)
    stat[...] = jnp.zeros_like(stat)

    chunk_base = counter[0]
    counter[0] += 4 * 7

    def send_chunk(chunk, start=True):
        copies = []
        for i, k in enumerate((4, 3, 5, 2, 6, 1, 7)):
            to = (t + k) % 8
            copies.append(
                remote(
                    num_b.at[chunk, pl.ds(to * 4, 4)],
                    rec_num.at[k, chunk],
                    (dp, to),
                    at=chunk_base + chunk * 7 + i,
                    start=start,
                )
            )
        return copies

    def attend(blk, lower):
        at = pl.multiple_of(blk * 8, 8)
        rows = pl.ds(at, 8)
        limit = jnp.zeros((1, 256), jnp.int32)
        for r in range(8):
            limit = jnp.where(lane_row == r, len_ref[at + r], limit)
        bias = jnp.where(lane_pos < limit, 0.0, LOW)
        stats = jnp.zeros((8, 128), F32)
        for kv in range(2):
            q = q_ref[rows, pl.ds(kv * 16, 16), :].astype(F32).reshape(128, 128)
            q = q * lax.rsqrt(jnp.mean(q * q, axis=1, keepdims=True) + EPS) * qg_ref[...]
            q = dot(shuffle, q.astype(BF16)).astype(BF16)
            nk = nk_ref[rows, kv, :].astype(F32)
            nk = nk * lax.rsqrt(jnp.mean(nk * nk, axis=1, keepdims=True) + EPS) * kg_ref[...]
            nk = nk.astype(BF16).astype(F32)
            nv = nv_ref[rows, kv, :].astype(F32)
            keys = kc_ref[rows, kv].reshape(256, 128)
            values = vc_ref[rows, kv].reshape(256, 128)
            score = lax.dot_general(
                q, keys, (((1,), (1,)), ((), ())), preferred_element_type=F32
            )
            score = jnp.where(own_block, score * scaling + bias, LOW)
            fresh = (q.astype(F32).reshape(16, 8, 128) * nk[None]).reshape(128, 128)
            fresh = jnp.sum(fresh, axis=1, keepdims=True) * scaling
            top = jnp.maximum(jnp.max(score, axis=1, keepdims=True), fresh)
            weight = jnp.exp(score - top).astype(BF16)
            new_weight = jnp.exp(fresh - top).astype(BF16).astype(F32) * first
            number = dot(weight, values)
            total = dot(weight, ones) + new_weight
            number = number.reshape(16, 8, 128) + new_weight.reshape(16, 8, 1) * nv[None]
            top = jnp.broadcast_to(top, (128, 128)).reshape(16, 8, 128)
            total = total.reshape(16, 8, 128)
            for i in range(16):
                head = kv * 16 + i
                num_f[head, lower : lower + 8, :] = number[i]
                column = 8 * (head // 4) + head % 4
                stats = jnp.where(lane == column, top[i], stats)
                stats = jnp.where(lane == column + 4, total[i], stats)
        stat[rows, :] = stats

    def attend_chunk(chunk, carry):
        attend(chunk * 2, 0)
        attend(chunk * 2 + 1, 8)
        num_b[chunk] = num_f[...].astype(BF16)
        send_chunk(chunk)
        return carry

    lax.fori_loop(0, 4, attend_chunk, 0)
    stat_t[...] = stat[...].T
    partials = []
    for k in (4, 3, 5, 2, 6, 1, 7):
        to = (t + k) % 8
        tile = pl.ds(pl.multiple_of(to * 8, 8), 8)
        partials.append(remote(stat_t.at[tile, :], rec_stat.at[k], (dp, to)))
    for chunk in range(4):
        partials += send_chunk(chunk, start=False)

    for copy in spread:
        copy.wait_recv()
    table = table_s[...]
    for k in range(1, 8):
        table = table + table_r[k]
    packed[z, x] = table
    spread = [
        remote(packed.at[z, x], packed.at[z, x], device(x=along("x", k))) for k in (1, 2, 3)
    ]
    for chunk in range(4):
        rec_num[0, chunk] = num_b[chunk, pl.ds(t * 4, 4)]
    rec_stat[0] = stat_t[pl.ds(pl.multiple_of(t * 8, 8), 8), :]
    row = iota((384, 384), 0)
    col = iota((384, 384), 1)
    zz, yy, xx, rest = row // 96, (row // 24) % 4, (row // 6) % 4, row % 6
    perm[0] = (col == xx * 96 + zz * 24 + yy * 6 + rest).astype(F32).astype(BF16)
    perm[1] = (col == yy * 96 + xx * 24 + zz * 6 + rest).astype(F32).astype(BF16)
    zz, yy, xx, rest = col // 96, (col // 24) % 4, (col // 6) % 4, col % 6
    perm_t[0] = (row == xx * 96 + zz * 24 + yy * 6 + rest).astype(F32).astype(BF16)
    perm_t[1] = (row == yy * 96 + xx * 24 + zz * 6 + rest).astype(F32).astype(BF16)

    for copy in partials:
        copy.wait_recv()
    for copy in spread:
        copy.wait_recv()
    spread = [remote(packed.at[z], packed.at[z], device(z=along("z", k))) for k in (1, 2, 3)]
    tops = [rec_stat[k][0:4] for k in range(8)]
    best = tops[0]
    for top in tops[1:]:
        best = jnp.maximum(best, top)
    scale = [jnp.exp(top - best) for top in tops]
    whole = scale[0] * rec_stat[0][4:8]
    for k in range(1, 8):
        whole = whole + scale[k] * rec_stat[k][4:8]
    coef[...] = jnp.zeros_like(coef)
    for k in range(8):
        coef[8 * k : 8 * k + 4, :] = scale[k] / whole
    columns = coef[...].T
    for j in range(4):
        out = jnp.zeros((64, 128), F32)
        for k in range(8):
            out = out + columns[0:64, 8 * k + j : 8 * k + j + 1] * rec_num[k, :, j].reshape(64, 128).astype(F32)
        attn[:, 128 * j : 128 * j + 128] = out.astype(BF16)

    weights[0].wait()
    pairs = []
    for j in (0, 1):
        for tile in (0, 1):
            cols = pl.ds(pl.multiple_of((1 - c) * HALF + j * 1024 + tile * 512, 512), 512)
            pair_s[j, :, tile * 512 : tile * 512 + 512] = dot(attn[...], wp[:, cols]).astype(BF16)
        pairs.append(remote(pair_s.at[j], pair_r.at[j], sibling))
    shares = []
    for j in (0, 1):
        for tile in (0, 1):
            cols = pl.ds(pl.multiple_of(c * HALF + j * 1024 + tile * 512, 512), 512)
            part = dot(attn[...], wp[:, cols])
            if tile == 0:
                pairs[j].wait_recv()
            at = slice(tile * 512, tile * 512 + 512)
            send_b[j, :, at] = (part + pair_r[j, :, at].astype(F32)).astype(BF16)
        for k in (2, 1, 3):
            to = along("y", k)
            rows = pl.ds(pl.multiple_of(to * 16, 16), 16)
            shares.append(remote(send_b.at[j, rows, :], rec_b.at[k, j], device(y=to)))

    for copy in spread:
        copy.wait_recv()
    for tile in range(8):
        for iz in range(4):
            for ix in range(4):
                rows8 = packed[iz, ix]
                if tile > 0:
                    rows8 = pltpu.roll(rows8, 128 - 16 * tile, 1)
                meta[iz, ix, tile // 2, tile % 2] = rows8
    before = iota((256, 256), 0)
    after = iota((256, 256), 1)
    earlier = ((before // 8 == after // 8) & (before < after)).astype(F32).astype(BF16)
    slot_base = ((iota((1, 256), 1) // 8) * 3).astype(F32)
    slot_id = iota((SLOTS, 256), 0).astype(F32)
    for p in range(3):
        a, b, last = ORDER[p]
        for ib in range(4):
            for ia in range(4):
                at = dict(here, **{a: ia, b: ib})
                plane_meta[pl.ds((ib * 4 + ia) * 16, 16), :] = meta[
                    at["z"], at["x"], at["y"]
                ].reshape(16, 128)
        table = plane_meta[...].T
        chosen, gates = table[0:8], table[8:16]
        for k in range(4):
            for core in range(2):
                at = dict(here, **{last: k, "c": core})
                expert = (at["z"] * 32 + at["x"] * 8 + at["y"] * 2 + at["c"]).astype(F32)
                hit = (chosen == expert).astype(F32)
                used = jnp.sum(hit, axis=0, keepdims=True)
                gate = jnp.sum(hit * gates, axis=0, keepdims=True)
                rank = dot(jnp.broadcast_to(used, (8, 256)).astype(BF16), earlier)[0:1]
                slot = jnp.where(used > 0.5, slot_base + rank, -1.0)
                match = slot == slot_id
                first_slot = (k * 2 + core) * SLOTS
                disp[p, first_slot : first_slot + SLOTS, :] = match.astype(F32).astype(BF16)
                comb[p, first_slot : first_slot + SLOTS, :] = jnp.where(match, gate, 0.0).astype(BF16)

    res_copy.wait_recv()
    for copy in shares:
        copy.wait_recv()
    rows = pl.ds(pl.multiple_of(y * 16, 16), 16)
    for j in (0, 1):
        total = send_b[j, rows, :].astype(F32)
        for k in (1, 2, 3):
            total = total + rec_b[k, j].astype(F32)
        at = slice(j * 1024, j * 1024 + 1024)
        hidden[:, at] = hidden[:, at] + total
    value = hidden[...]
    squares = jnp.sum(value * value, axis=1, keepdims=True)
    sq_own[...] = jnp.broadcast_to(squares, (16, 128))
    sq_copy = remote(sq_own, sq_rec, sibling)
    sq_copy.wait_recv()
    mean = (squares + sq_rec[:, 0:1]) * (1.0 / D)
    normed = (value * lax.rsqrt(mean + EPS) * ng_ref[:, own_cols]).astype(BF16)

    stage = {}
    for wave in FORTH:
        for p in wave:
            order, first, width = PARTS[p]
            a, b, last = ORDER[order]
            g[p][here[b], here[a]] = normed[:, first : first + width]
            unit = g[p].at[here[b], here[a]]
            stage[p] = [remote(unit, unit, device(**{a: along(a, k)})) for k in (2, 1, 3)]
    for wave in FORTH:
        for p in wave:
            a, b, last = ORDER[PARTS[p][0]]
            for copy in stage[p]:
                copy.wait_recv()
            unit = g[p].at[here[b]]
            stage[p] = [remote(unit, unit, device(**{b: along(b, k)})) for k in (2, 1, 3)]
    locals_in = {}
    for wave in FORTH:
        for p in wave:
            order, first, width = PARTS[p]
            a, b, last = ORDER[order]
            for copy in stage[p]:
                copy.wait_recv()
            plane = g[p][...].reshape(256, width)
            stage[p] = []
            for k in (2, 1, 3, 0):
                to = along(last, k)
                wanted = pl.ds(pl.multiple_of(to * 2 * SLOTS, 2 * SLOTS), 2 * SLOTS)
                picked = dot(disp[order, wanted, :], plane)
                xs[p][k] = picked.astype(BF16).reshape(2, SLOTS, width)
                for j in (1, 0):
                    core = (c + j) % 2
                    src = xs[p].at[k, core]
                    dst = xr[p].at[c, here[last]]
                    if k == 0 and j == 0:
                        local = pltpu.make_async_copy(src, dst, loc_sem.at[p])
                        local.start()
                        locals_in[p] = local
                    else:
                        stage[p].append(remote(src, dst, device(**{last: to, "c": core})))
    for n, wave in enumerate(FORTH):
        for p in wave:
            order, first, width = PARTS[p]
            for copy in stage[p]:
                copy.wait_recv()
            locals_in[p].wait()
            for half in (0, 1):
                block = xr[p][half].reshape(384, width)
                if order > 0:
                    block = dot(perm[order - 1], block).astype(BF16)
                x_full[:, half * HALF + first : half * HALF + first + width] = block
        if n == 0:
            for copy in weights[1:]:
                copy.wait()
        low = min(PARTS[p][1] for p in wave)
        high = max(PARTS[p][1] + PARTS[p][2] for p in wave)

        def expert(i, carry, n=n, low=low, high=high):
            cols = pl.ds(pl.multiple_of(i * 256, 256), 256)
            sums = []
            for which, weight in ((0, wg), (1, wu)):
                total = dot(x_full[:, low:high], weight[low:high, cols])
                total = total + dot(
                    x_full[:, HALF + low : HALF + high], weight[HALF + low : HALF + high, cols]
                )
                if n > 0:
                    total = total + acc[which, :, cols]
                if n < len(FORTH) - 1:
                    acc[which, :, cols] = total
                sums.append(total)
            if n == len(FORTH) - 1:
                gate, up = sums
                act[:, cols] = (gate / (1.0 + jnp.exp(-gate)) * up).astype(BF16)
            return carry

        lax.fori_loop(0, FFW // 256, expert, 0)

    stage, locals_out, ready = {}, {}, []
    for wave in BACK:
        for p in wave:
            order, first, width = PARTS[p]
            a, b, last = ORDER[order]
            if order == 0:
                turned = act
            else:
                turned = act_p.at[order - 1]
                if order not in ready:
                    ready.append(order)
                    turned[...] = dot(perm_t[order - 1], act[...]).astype(BF16)
            stage[p] = []
            for j in (1, 0):
                core = (c + j) % 2
                cols = pl.ds(pl.multiple_of(core * HALF + first, 128), width)
                result = dot(turned[...], wd[:, cols])
                ys[p][j] = result.astype(BF16).reshape(4, SLOTS, width)
                for k in (2, 1, 3, 0):
                    to = along(last, k)
                    src = ys[p].at[j, to]
                    dst = yr[p].at[here[last] * 2 + c]
                    if k == 0 and j == 0:
                        local = pltpu.make_async_copy(src, dst, loc_sem.at[len(PARTS) + p])
                        local.start()
                        locals_out[p] = local
                    else:
                        stage[p].append(remote(src, dst, device(**{last: to, "c": core})))
    for wave in BACK:
        for p in wave:
            order, first, width = PARTS[p]
            a, b, last = ORDER[order]
            for copy in stage[p]:
                copy.wait_recv()
            locals_out[p].wait()
            summed = lax.dot_general(
                comb[order], yr[p][...].reshape(8 * SLOTS, width), (((0,), (0,)), ((), ())),
                preferred_element_type=F32,
            )
            ps[p][...] = summed.astype(BF16).reshape(4, 64, width)
            stage[p] = []
            for k in (2, 1, 3):
                to = along(b, k)
                stage[p].append(remote(ps[p].at[to], rb[p].at[k], device(**{b: to})))
        for p in wave:
            order, first, width = PARTS[p]
            a, b, last = ORDER[order]
            for copy in stage[p]:
                copy.wait_recv()
            total = ps[p][here[b]].astype(F32)
            for k in (1, 2, 3):
                total = total + rb[p][k].astype(F32)
            ra_s[p][...] = total.astype(BF16).reshape(4, 16, width)
            stage[p] = []
            for k in (2, 1, 3):
                to = along(a, k)
                stage[p].append(remote(ra_s[p].at[to], ra_r[p].at[k], device(**{a: to})))
    for wave in BACK:
        for p in wave:
            order, first, width = PARTS[p]
            a, b, last = ORDER[order]
            for copy in stage[p]:
                copy.wait_recv()
            total = ra_s[p][here[a]].astype(F32)
            for k in (1, 2, 3):
                total = total + ra_r[p][k].astype(F32)
            cols = slice(first, first + width)
            hidden[:, cols] = hidden[:, cols] + total

    fin_s[1] = hidden[other_rows, :]
    fin = remote(fin_s.at[1], fin_r, sibling)
    out_ref[:, own_cols] = hidden[own_rows, :].astype(BF16)
    fin.wait_recv()
    out_ref[:, other_cols] = fin_r[...].astype(BF16)
    for copy in sent:
        copy.wait_send()


COPIES = 1 + 7 + 28 + 7 + 3 + 3 + 2 + 6 + 1 + 1 + len(PARTS) * (3 + 3 + 7 + 7 + 3 + 3)


def shards(
    queries, new_keys, new_values, key_cache, value_cache, lengths, residual_in, query_gain, key_gain,
    out_proj, norm_gain, expert_ids, gate_weights, expert_gate, expert_up, expert_down,
):
    vmem = pl.BlockSpec(memory_space=pltpu.VMEM)
    anywhere = pl.BlockSpec(memory_space=pl.ANY)

    def each(shape_of):
        return [VMEM(shape_of(width), BF16) for _, _, width in PARTS]

    return pl.pallas_call(
        kernel,
        out_shape=jax.ShapeDtypeStruct((8, D), BF16),
        in_specs=[vmem] * 5 + [pl.BlockSpec(memory_space=pltpu.SMEM)] + [vmem] * 6 + [anywhere] * 4,
        out_specs=vmem,
        scratch_shapes=[
            VMEM((512, D), BF16), VMEM((D, FFW), BF16), VMEM((D, FFW), BF16), VMEM((FFW, D), BF16),
            VMEM((32, 16, 128), F32), VMEM((4, 32, 16, 128), BF16), VMEM((128, 128), F32),
            VMEM((128, 128), F32), VMEM((128, 128), F32), VMEM((8, 4, 4, 16, 128), BF16),
            VMEM((8, 8, 128), F32), VMEM((64, 512), BF16),
            VMEM((2, 64, 1024), BF16), VMEM((2, 64, 1024), BF16), VMEM((2, 64, 1024), BF16),
            VMEM((4, 2, 16, 1024), BF16), VMEM((16, HALF), F32),
            VMEM((16, 128), F32), VMEM((16, 128), F32),
            VMEM((8, 128), F32), VMEM((8, 8, 128), F32), VMEM((4, 4, 8, 128), F32),
            VMEM((4, 4, 4, 2, 8, 128), F32), VMEM((256, 128), F32),
            VMEM((3, 8 * SLOTS, 256), BF16), VMEM((3, 8 * SLOTS, 256), BF16),
            VMEM((384, D), BF16), VMEM((2, 384, 384), BF16), VMEM((2, 384, 384), BF16),
            VMEM((2, 384, FFW), F32), VMEM((384, FFW), BF16), VMEM((2, 384, FFW), BF16),
            each(lambda w: (4, 4, 16, w)),
            each(lambda w: (4, 2, SLOTS, w)),
            each(lambda w: (2, 4, SLOTS, w)),
            each(lambda w: (2, 4, SLOTS, w)),
            each(lambda w: (8, SLOTS, w)),
            each(lambda w: (4, 64, w)), each(lambda w: (4, 64, w)),
            each(lambda w: (4, 16, w)), each(lambda w: (4, 16, w)),
            VMEM((2, 8, HALF), F32), VMEM((8, HALF), F32),
            pltpu.SemaphoreType.DMA((4,)), pltpu.SemaphoreType.DMA((2 * len(PARTS),)),
            pltpu.SemaphoreType.DMA((COPIES,)), pltpu.SemaphoreType.DMA((COPIES,)),
        ],
        compiler_params=pltpu.CompilerParams(
            collective_id=0, has_side_effects=True, vmem_limit_bytes=60 * 2**20
        ),
        cost_estimate=pl.CostEstimate(flops=10**10, bytes_accessed=26 * 2**20, transcendentals=10**6),
    )(
        queries, new_keys, new_values, key_cache, value_cache, lengths, residual_in,
        query_gain.reshape(1, 128), key_gain.reshape(1, 128), norm_gain.reshape(1, D),
        expert_ids, gate_weights, out_proj, expert_gate, expert_up, expert_down,
    )


def solution(mesh):
    rows = P(("dp", "tensor"), None)
    experts = P(("dp", "tensor"), None, None)
    cache = P("dp", None, "tensor", None)
    heads = P("dp", None, None)
    return jax.shard_map(
        shards,
        mesh=mesh,
        in_specs=(
            heads, heads, heads, cache, cache, P("dp"), rows, P(), P(),
            P("tensor", None), P(), rows, rows, experts, experts, experts,
        ),
        out_specs=rows,
        check_vma=False,
    )
```

```python
import jax
import jax.numpy as jnp
from jax import lax
from jax.experimental import pallas as pl
from jax.experimental.pallas import tpu as pltpu
from jax.sharding import PartitionSpec as P

MESH = pl.DeviceIdType.MESH
F32 = jnp.float32
BF16 = jnp.bfloat16
VMEM = pltpu.VMEM

D = 4096
HALF = 2048
FFW = 768
SLOTS = 96
EPS = 1e-6
LOW = -1e30
ORDER = (("x", "y", "z"), ("y", "z", "x"), ("z", "x", "y"))
WAVES = (((2, 0, 384), (0, 384, 256), (1, 640, 384)), ((2, 1024, 384), (0, 1408, 384), (1, 1792, 256)))
PARTS = tuple(part for wave in WAVES for part in wave)
FORTH = ((0, 1, 2), (3, 4, 5))
BACK = ((3, 4, 5), (0, 1, 2))


def iota(shape, dim):
    return lax.broadcasted_iota(jnp.int32, shape, dim)


def dot(a, b):
    return jnp.dot(a, b, preferred_element_type=F32)


def kernel(
    q_hbm, nk_hbm, nv_hbm, kc_hbm, vc_hbm, len_hbm, res_hbm, qg_hbm, kg_hbm, ng_hbm, ids_hbm, gw_hbm,
    wp_hbm, wg_hbm, wu_hbm, wd_hbm,
    out_ref,
    q_ref, nk_ref, nv_ref, kc_ref, vc_ref, len_ref, res_ref, qg_ref, kg_ref, ng_ref, ids_ref, gw_ref,
    wp, wg, wu, wd,
    num_f, num_b, stat, stat_t, coef, rec_num, rec_stat, attn,
    pair_s, pair_r, send_b, rec_b, hidden, sq_own, sq_rec,
    table_s, table_r, packed, meta, plane_meta, disp, comb,
    x_full, perm, perm_t, acc, act, act_p,
    g, xs, xr, ys, yr, ps, rb, ra_s, ra_r,
    fin_s, fin_r,
    in_sem, w_sem, loc_sem, send_sem, recv_sem,
):
    dp = lax.axis_index("dp")
    t = lax.axis_index("tensor")
    here = {"z": dp // 4, "x": dp % 4, "y": t // 2, "c": t % 2}
    c = here["c"]

    def device(**moved):
        at = dict(here, **moved)
        return (at["z"] * 4 + at["x"], at["y"] * 2 + at["c"])

    def along(axis, k):
        return (here[axis] + k) % 4

    def tensor_peer(k):
        return (dp, (t + k) % 8)

    counter = [0]
    groups = []

    class Group:
        def __init__(self, like):
            self.index = counter[0]
            counter[0] += 1
            self.like = like
            groups.append(self)

        def copy(self, src, dst, to):
            return pltpu.make_async_remote_copy(
                src_ref=src,
                dst_ref=dst,
                send_sem=send_sem.at[self.index],
                recv_sem=recv_sem.at[self.index],
                device_id=to,
                device_id_type=MESH,
            )

        def send(self, src, dst, to):
            self.copy(src, dst, to).start()

        def wait_recv(self):
            self.copy(self.like, self.like, sibling).wait_recv()

        def wait_send(self):
            self.copy(self.like, self.like, sibling).wait_send()

    def remote(src, dst, to):
        group = Group(src)
        group.send(src, dst, to)
        return group

    sibling = device(c=1 - c)
    own_rows = pl.ds(pl.multiple_of(c * 8, 8), 8)
    other_rows = pl.ds(pl.multiple_of((1 - c) * 8, 8), 8)
    own_cols = pl.ds(pl.multiple_of(c * HALF, HALF), HALF)
    other_cols = pl.ds(pl.multiple_of((1 - c) * HALF, HALF), HALF)

    barrier = pltpu.get_barrier_semaphore()
    peers = [tensor_peer(k) for k in range(1, 8)]
    for axis in ("x", "z"):
        for k in (1, 2, 3):
            for core in (0, 1):
                peers.append(device(**{axis: along(axis, k), "c": core}))
    for peer in peers:
        pl.semaphore_signal(barrier, inc=1, device_id=peer, device_id_type=MESH)

    inputs = []
    for i, (src, dst) in enumerate(
        (
            (q_hbm, q_ref), (kc_hbm, kc_ref), (vc_hbm, vc_ref), (nk_hbm, nk_ref), (nv_hbm, nv_ref),
            (len_hbm, len_ref), (qg_hbm, qg_ref), (kg_hbm, kg_ref), (ids_hbm, ids_ref),
            (gw_hbm, gw_ref), (res_hbm, res_ref), (ng_hbm, ng_ref),
        )
    ):
        inputs.append(pltpu.make_async_copy(src, dst, in_sem.at[i]))
        inputs[-1].start()
    scaling = 128.0**-0.5
    first = (t == 0).astype(F32)
    shuffle = (iota((128, 128), 1) == (iota((128, 128), 0) % 8) * 16 + iota((128, 128), 0) // 8)
    shuffle = shuffle.astype(F32).astype(BF16)
    lane_row = iota((1, 256), 1) // 32
    lane_pos = iota((1, 256), 1) % 32 + t * 32
    own_block = (iota((128, 256), 0) % 8) == (iota((128, 256), 1) // 32)
    ones = jnp.ones((256, 128), BF16)
    lane = iota((8, 128), 1)
    stat[...] = jnp.zeros_like(stat)

    shares_a = Group(rec_num.at[pl.ds(1, 7)])

    def send_chunk(chunk):
        for k in (4, 3, 5, 2, 6, 1, 7):
            to = (t + k) % 8
            shares_a.send(num_b.at[chunk, pl.ds(to * 4, 4)], rec_num.at[k, chunk], (dp, to))

    def attend(blk, lower):
        at = pl.multiple_of(blk * 8, 8)
        rows = pl.ds(at, 8)
        limit = jnp.zeros((1, 256), jnp.int32)
        for r in range(8):
            limit = jnp.where(lane_row == r, len_ref[at + r], limit)
        bias = jnp.where(lane_pos < limit, 0.0, LOW)
        stats = jnp.zeros((8, 128), F32)
        for kv in range(2):
            q = q_ref[rows, pl.ds(kv * 16, 16), :].astype(F32).reshape(128, 128)
            q = q * lax.rsqrt(jnp.mean(q * q, axis=1, keepdims=True) + EPS) * qg_ref[...]
            q = dot(shuffle, q.astype(BF16)).astype(BF16)
            nk = nk_ref[rows, kv, :].astype(F32)
            nk = nk * lax.rsqrt(jnp.mean(nk * nk, axis=1, keepdims=True) + EPS) * kg_ref[...]
            nk = nk.astype(BF16).astype(F32)
            nv = nv_ref[rows, kv, :].astype(F32)
            keys = kc_ref[rows, kv].reshape(256, 128)
            values = vc_ref[rows, kv].reshape(256, 128)
            score = lax.dot_general(
                q, keys, (((1,), (1,)), ((), ())), preferred_element_type=F32
            )
            score = jnp.where(own_block, score * scaling + bias, LOW)
            fresh = (q.astype(F32).reshape(16, 8, 128) * nk[None]).reshape(128, 128)
            fresh = jnp.sum(fresh, axis=1, keepdims=True) * scaling
            top = jnp.maximum(jnp.max(score, axis=1, keepdims=True), fresh)
            weight = jnp.exp(score - top).astype(BF16)
            new_weight = jnp.exp(fresh - top).astype(BF16).astype(F32) * first
            number = dot(weight, values)
            total = dot(weight, ones) + new_weight
            number = number.reshape(16, 8, 128) + new_weight.reshape(16, 8, 1) * nv[None]
            top = jnp.broadcast_to(top, (128, 128)).reshape(16, 8, 128)
            total = total.reshape(16, 8, 128)
            for i in range(16):
                head = kv * 16 + i
                num_f[head, lower : lower + 8, :] = number[i]
                column = 8 * (head // 4) + head % 4
                stats = jnp.where(lane == column, top[i], stats)
                stats = jnp.where(lane == column + 4, total[i], stats)
        stat[rows, :] = stats

    def attend_chunk(chunk):
        attend(chunk * 2, 0)
        attend(chunk * 2 + 1, 8)
        num_b[chunk] = num_f[...].astype(BF16)

    for copy in inputs[:8]:
        copy.wait()
    weights = [pltpu.make_async_copy(wp_hbm, wp, w_sem.at[0])]
    weights[0].start()
    attend_chunk(0)
    pl.semaphore_wait(barrier, len(peers))
    send_chunk(0)

    for copy in inputs[8:]:
        copy.wait()
    gw = gw_ref[...]
    route = (gw / jnp.sum(gw, axis=1, keepdims=True)).astype(BF16)
    put = iota((8, 128), 1) - iota((8, 128), 0) - t * 16
    ids = ids_ref[...].astype(F32).astype(BF16)
    table = dot(ids, (put == 0).astype(F32).astype(BF16)) + dot(
        route, (put == 8).astype(F32).astype(BF16)
    )
    z, x, y = here["z"], here["x"], here["y"]
    table_s[...] = table
    spread = Group(table_r.at[pl.ds(1, 7)])
    for k in range(1, 8):
        spread.send(table_s, table_r.at[k], tensor_peer(k))

    hidden[own_rows, :] = res_ref[:, own_cols].astype(F32)
    fin_s[0] = res_ref[:, other_cols].astype(F32)
    res_copy = remote(fin_s.at[0], hidden.at[own_rows, :], sibling)

    def attend_more(chunk, carry):
        attend_chunk(chunk)
        send_chunk(chunk)
        return carry

    lax.fori_loop(1, 4, attend_more, 0)
    stat_t[...] = stat[...].T
    tops_a = Group(rec_stat.at[pl.ds(1, 7)])
    for k in (4, 3, 5, 2, 6, 1, 7):
        to = (t + k) % 8
        tile = pl.ds(pl.multiple_of(to * 8, 8), 8)
        tops_a.send(stat_t.at[tile, :], rec_stat.at[k], (dp, to))

    spread.wait_recv()
    table = table_s[...]
    for k in range(1, 8):
        table = table + table_r[k]
    packed[z, x] = table
    spread = Group(packed.at[z, pl.ds(0, 3)])
    for k in (1, 2, 3):
        spread.send(packed.at[z, x], packed.at[z, x], device(x=along("x", k)))
    for chunk in range(4):
        rec_num[0, chunk] = num_b[chunk, pl.ds(t * 4, 4)]
    rec_stat[0] = stat_t[pl.ds(pl.multiple_of(t * 8, 8), 8), :]
    for i, (src, dst) in enumerate(((wg_hbm, wg), (wu_hbm, wu), (wd_hbm, wd))):
        weights.append(pltpu.make_async_copy(src.at[0], dst, w_sem.at[1 + i]))
        weights[-1].start()
    row = iota((384, 384), 0)
    col = iota((384, 384), 1)
    zz, yy, xx, rest = row // 96, (row // 24) % 4, (row // 6) % 4, row % 6
    perm[0] = (col == xx * 96 + zz * 24 + yy * 6 + rest).astype(F32).astype(BF16)
    perm[1] = (col == yy * 96 + xx * 24 + zz * 6 + rest).astype(F32).astype(BF16)
    zz, yy, xx, rest = col // 96, (col // 24) % 4, (col // 6) % 4, col % 6
    perm_t[0] = (row == xx * 96 + zz * 24 + yy * 6 + rest).astype(F32).astype(BF16)
    perm_t[1] = (row == yy * 96 + xx * 24 + zz * 6 + rest).astype(F32).astype(BF16)

    tops_a.wait_recv()
    shares_a.wait_recv()
    spread.wait_recv()
    spread = Group(packed.at[pl.ds(0, 3)])
    for k in (1, 2, 3):
        spread.send(packed.at[z], packed.at[z], device(z=along("z", k)))
    tops = [rec_stat[k][0:4] for k in range(8)]
    best = tops[0]
    for top in tops[1:]:
        best = jnp.maximum(best, top)
    scale = [jnp.exp(top - best) for top in tops]
    whole = scale[0] * rec_stat[0][4:8]
    for k in range(1, 8):
        whole = whole + scale[k] * rec_stat[k][4:8]
    coef[...] = jnp.zeros_like(coef)
    for k in range(8):
        coef[8 * k : 8 * k + 4, :] = scale[k] / whole
    columns = coef[...].T
    for j in range(4):
        out = jnp.zeros((64, 128), F32)
        for k in range(8):
            out = out + columns[0:64, 8 * k + j : 8 * k + j + 1] * rec_num[k, :, j].reshape(64, 128).astype(F32)
        attn[:, 128 * j : 128 * j + 128] = out.astype(BF16)

    weights[0].wait()
    pairs = []
    for j in (0, 1):
        for tile in (0, 1):
            cols = pl.ds(pl.multiple_of((1 - c) * HALF + j * 1024 + tile * 512, 512), 512)
            pair_s[j, :, tile * 512 : tile * 512 + 512] = dot(attn[...], wp[:, cols]).astype(BF16)
        pairs.append(remote(pair_s.at[j], pair_r.at[j], sibling))
    shares = Group(rec_b.at[pl.ds(1, 3)])
    for j in (0, 1):
        for tile in (0, 1):
            cols = pl.ds(pl.multiple_of(c * HALF + j * 1024 + tile * 512, 512), 512)
            part = dot(attn[...], wp[:, cols])
            if tile == 0:
                pairs[j].wait_recv()
            at = slice(tile * 512, tile * 512 + 512)
            send_b[j, :, at] = (part + pair_r[j, :, at].astype(F32)).astype(BF16)
        for k in (2, 1, 3):
            to = along("y", k)
            rows = pl.ds(pl.multiple_of(to * 16, 16), 16)
            shares.send(send_b.at[j, rows, :], rec_b.at[k, j], device(y=to))

    spread.wait_recv()
    for tile in range(8):
        for iz in range(4):
            for ix in range(4):
                rows8 = packed[iz, ix]
                if tile > 0:
                    rows8 = pltpu.roll(rows8, 128 - 16 * tile, 1)
                meta[iz, ix, tile // 2, tile % 2] = rows8
    before = iota((256, 256), 0)
    after = iota((256, 256), 1)
    earlier = ((before // 8 == after // 8) & (before < after)).astype(F32).astype(BF16)
    slot_base = ((iota((1, 256), 1) // 8) * 3).astype(F32)
    slot_id = iota((SLOTS, 256), 0).astype(F32)
    for p in range(3):
        a, b, last = ORDER[p]
        for ib in range(4):
            for ia in range(4):
                at = dict(here, **{a: ia, b: ib})
                plane_meta[pl.ds((ib * 4 + ia) * 16, 16), :] = meta[
                    at["z"], at["x"], at["y"]
                ].reshape(16, 128)
        table = plane_meta[...].T
        chosen, gates = table[0:8], table[8:16]
        for k in range(4):
            for core in range(2):
                at = dict(here, **{last: k, "c": core})
                expert = (at["z"] * 32 + at["x"] * 8 + at["y"] * 2 + at["c"]).astype(F32)
                hit = (chosen == expert).astype(F32)
                used = jnp.sum(hit, axis=0, keepdims=True)
                gate = jnp.sum(hit * gates, axis=0, keepdims=True)
                rank = dot(jnp.broadcast_to(used, (8, 256)).astype(BF16), earlier)[0:1]
                slot = jnp.where(used > 0.5, slot_base + rank, -1.0)
                match = slot == slot_id
                first_slot = (k * 2 + core) * SLOTS
                disp[p, first_slot : first_slot + SLOTS, :] = match.astype(F32).astype(BF16)
                comb[p, first_slot : first_slot + SLOTS, :] = jnp.where(match, gate, 0.0).astype(BF16)

    res_copy.wait_recv()
    shares.wait_recv()
    rows = pl.ds(pl.multiple_of(y * 16, 16), 16)
    for j in (0, 1):
        total = send_b[j, rows, :].astype(F32)
        for k in (1, 2, 3):
            total = total + rec_b[k, j].astype(F32)
        at = slice(j * 1024, j * 1024 + 1024)
        hidden[:, at] = hidden[:, at] + total
    value = hidden[...]
    squares = jnp.sum(value * value, axis=1, keepdims=True)
    sq_own[...] = jnp.broadcast_to(squares, (16, 128))
    sq_copy = remote(sq_own, sq_rec, sibling)
    sq_copy.wait_recv()
    mean = (squares + sq_rec[:, 0:1]) * (1.0 / D)
    normed = (value * lax.rsqrt(mean + EPS) * ng_ref[:, own_cols]).astype(BF16)

    stage = {}
    for wave in FORTH:
        for p in wave:
            order, first, width = PARTS[p]
            a, b, last = ORDER[order]
            g[p][here[b], here[a]] = normed[:, first : first + width]
            unit = g[p].at[here[b], here[a]]
            stage[p] = Group(g[p].at[here[b], pl.ds(0, 3)])
            for k in (2, 1, 3):
                stage[p].send(unit, unit, device(**{a: along(a, k)}))
    for wave in FORTH:
        for p in wave:
            a, b, last = ORDER[PARTS[p][0]]
            stage[p].wait_recv()
            unit = g[p].at[here[b]]
            stage[p] = Group(g[p].at[pl.ds(0, 3)])
            for k in (2, 1, 3):
                stage[p].send(unit, unit, device(**{b: along(b, k)}))
    locals_in = {}
    for wave in FORTH:
        for p in wave:
            order, first, width = PARTS[p]
            a, b, last = ORDER[order]
            stage[p].wait_recv()
            plane = g[p][...].reshape(256, width)
            stage[p] = Group(xs[p].at[pl.ds(0, 7)])
            for k in (2, 1, 3, 0):
                to = along(last, k)
                wanted = pl.ds(pl.multiple_of(to * 2 * SLOTS, 2 * SLOTS), 2 * SLOTS)
                picked = dot(disp[order, wanted, :], plane)
                xs[p][2 * k : 2 * k + 2] = picked.astype(BF16).reshape(2, SLOTS, width)
                for j in (1, 0):
                    core = (c + j) % 2
                    src = xs[p].at[2 * k + core]
                    dst = xr[p].at[c, here[last]]
                    if k == 0 and j == 0:
                        local = pltpu.make_async_copy(src, dst, loc_sem.at[p])
                        local.start()
                        locals_in[p] = local
                    else:
                        stage[p].send(src, dst, device(**{last: to, "c": core}))
    for n, wave in enumerate(FORTH):
        for p in wave:
            order, first, width = PARTS[p]
            stage[p].wait_recv()
            locals_in[p].wait()
            for half in (0, 1):
                block = xr[p][half].reshape(384, width)
                if order > 0:
                    block = dot(perm[order - 1], block).astype(BF16)
                x_full[:, half * HALF + first : half * HALF + first + width] = block
        if n == 0:
            for copy in weights[1:]:
                copy.wait()
        low = min(PARTS[p][1] for p in wave)
        high = max(PARTS[p][1] + PARTS[p][2] for p in wave)

        def expert(i, carry, n=n, low=low, high=high):
            cols = pl.ds(pl.multiple_of(i * 256, 256), 256)
            sums = []
            for which, weight in ((0, wg), (1, wu)):
                total = dot(x_full[:, low:high], weight[low:high, cols])
                total = total + dot(
                    x_full[:, HALF + low : HALF + high], weight[HALF + low : HALF + high, cols]
                )
                if n > 0:
                    total = total + acc[which, :, cols]
                if n < len(FORTH) - 1:
                    acc[which, :, cols] = total
                sums.append(total)
            if n == len(FORTH) - 1:
                gate, up = sums
                act[:, cols] = (gate / (1.0 + jnp.exp(-gate)) * up).astype(BF16)
            return carry

        lax.fori_loop(0, FFW // 256, expert, 0)

    stage, locals_out, ready = {}, {}, []
    for wave in BACK:
        for p in wave:
            order, first, width = PARTS[p]
            a, b, last = ORDER[order]
            if order == 0:
                turned = act
            else:
                turned = act_p.at[order - 1]
                if order not in ready:
                    ready.append(order)
                    turned[...] = dot(perm_t[order - 1], act[...]).astype(BF16)
            stage[p] = Group(ys[p].at[pl.ds(0, 7)])
            for j in (1, 0):
                core = (c + j) % 2
                cols = pl.ds(pl.multiple_of(core * HALF + first, 128), width)
                result = dot(turned[...], wd[:, cols])
                ys[p][4 * j : 4 * j + 4] = result.astype(BF16).reshape(4, SLOTS, width)
                for k in (2, 1, 3, 0):
                    to = along(last, k)
                    src = ys[p].at[4 * j + to]
                    dst = yr[p].at[here[last] * 2 + c]
                    if k == 0 and j == 0:
                        local = pltpu.make_async_copy(src, dst, loc_sem.at[len(PARTS) + p])
                        local.start()
                        locals_out[p] = local
                    else:
                        stage[p].send(src, dst, device(**{last: to, "c": core}))
    for wave in BACK:
        for p in wave:
            order, first, width = PARTS[p]
            a, b, last = ORDER[order]
            stage[p].wait_recv()
            locals_out[p].wait()
            summed = lax.dot_general(
                comb[order], yr[p][...].reshape(8 * SLOTS, width), (((0,), (0,)), ((), ())),
                preferred_element_type=F32,
            )
            ps[p][...] = summed.astype(BF16).reshape(4, 64, width)
            stage[p] = Group(ps[p].at[pl.ds(0, 3)])
            for k in (2, 1, 3):
                to = along(b, k)
                stage[p].send(ps[p].at[to], rb[p].at[k], device(**{b: to}))
        for p in wave:
            order, first, width = PARTS[p]
            a, b, last = ORDER[order]
            stage[p].wait_recv()
            total = ps[p][here[b]].astype(F32)
            for k in (1, 2, 3):
                total = total + rb[p][k].astype(F32)
            ra_s[p][...] = total.astype(BF16).reshape(4, 16, width)
            stage[p] = Group(ra_s[p].at[pl.ds(0, 3)])
            for k in (2, 1, 3):
                to = along(a, k)
                stage[p].send(ra_s[p].at[to], ra_r[p].at[k], device(**{a: to}))
    for wave in BACK:
        for p in wave:
            order, first, width = PARTS[p]
            a, b, last = ORDER[order]
            stage[p].wait_recv()
            total = ra_s[p][here[a]].astype(F32)
            for k in (1, 2, 3):
                total = total + ra_r[p][k].astype(F32)
            cols = slice(first, first + width)
            hidden[:, cols] = hidden[:, cols] + total

    fin_s[1] = hidden[other_rows, :]
    fin = remote(fin_s.at[1], fin_r, sibling)
    out_ref[:, own_cols] = hidden[own_rows, :].astype(BF16)
    fin.wait_recv()
    out_ref[:, other_cols] = fin_r[...].astype(BF16)
    for group in groups:
        group.wait_send()


GROUPS = 11 + 6 * len(PARTS)


def shards(
    queries, new_keys, new_values, key_cache, value_cache, lengths, residual_in, query_gain, key_gain,
    out_proj, norm_gain, expert_ids, gate_weights, expert_gate, expert_up, expert_down,
):
    anywhere = pl.BlockSpec(memory_space=pl.ANY)

    def each(shape_of):
        return [VMEM(shape_of(width), BF16) for _, _, width in PARTS]

    return pl.pallas_call(
        kernel,
        out_shape=jax.ShapeDtypeStruct((8, D), BF16),
        in_specs=[anywhere] * 16,
        out_specs=pl.BlockSpec(memory_space=pltpu.VMEM),
        scratch_shapes=[
            VMEM((64, 32, 128), BF16), VMEM((64, 2, 128), BF16), VMEM((64, 2, 128), BF16),
            VMEM((64, 2, 32, 128), BF16), VMEM((64, 2, 32, 128), BF16), pltpu.SMEM((64,), jnp.int32),
            VMEM((8, D), BF16), VMEM((1, 128), F32), VMEM((1, 128), F32), VMEM((1, D), F32),
            VMEM((8, 8), jnp.int32), VMEM((8, 8), F32),
            VMEM((512, D), BF16), VMEM((D, FFW), BF16), VMEM((D, FFW), BF16), VMEM((FFW, D), BF16),
            VMEM((32, 16, 128), F32), VMEM((4, 32, 16, 128), BF16), VMEM((128, 128), F32),
            VMEM((128, 128), F32), VMEM((128, 128), F32), VMEM((8, 4, 4, 16, 128), BF16),
            VMEM((8, 8, 128), F32), VMEM((64, 512), BF16),
            VMEM((2, 64, 1024), BF16), VMEM((2, 64, 1024), BF16), VMEM((2, 64, 1024), BF16),
            VMEM((4, 2, 16, 1024), BF16), VMEM((16, HALF), F32),
            VMEM((16, 128), F32), VMEM((16, 128), F32),
            VMEM((8, 128), F32), VMEM((8, 8, 128), F32), VMEM((4, 4, 8, 128), F32),
            VMEM((4, 4, 4, 2, 8, 128), F32), VMEM((256, 128), F32),
            VMEM((3, 8 * SLOTS, 256), BF16), VMEM((3, 8 * SLOTS, 256), BF16),
            VMEM((384, D), BF16), VMEM((2, 384, 384), BF16), VMEM((2, 384, 384), BF16),
            VMEM((2, 384, FFW), F32), VMEM((384, FFW), BF16), VMEM((2, 384, FFW), BF16),
            each(lambda w: (4, 4, 16, w)),
            each(lambda w: (8, SLOTS, w)),
            each(lambda w: (2, 4, SLOTS, w)),
            each(lambda w: (8, SLOTS, w)),
            each(lambda w: (8, SLOTS, w)),
            each(lambda w: (4, 64, w)), each(lambda w: (4, 64, w)),
            each(lambda w: (4, 16, w)), each(lambda w: (4, 16, w)),
            VMEM((2, 8, HALF), F32), VMEM((8, HALF), F32),
            pltpu.SemaphoreType.DMA((12,)), pltpu.SemaphoreType.DMA((4,)), pltpu.SemaphoreType.DMA((2 * len(PARTS),)),
            pltpu.SemaphoreType.DMA((GROUPS,)), pltpu.SemaphoreType.DMA((GROUPS,)),
        ],
        compiler_params=pltpu.CompilerParams(
            collective_id=0, has_side_effects=True, vmem_limit_bytes=60 * 2**20
        ),
        cost_estimate=pl.CostEstimate(flops=10**10, bytes_accessed=26 * 2**20, transcendentals=10**6),
    )(
        queries, new_keys, new_values, key_cache, value_cache, lengths, residual_in,
        query_gain.reshape(1, 128), key_gain.reshape(1, 128), norm_gain.reshape(1, D),
        expert_ids, gate_weights, out_proj, expert_gate, expert_up, expert_down,
    )


def solution(mesh):
    rows = P(("dp", "tensor"), None)
    experts = P(("dp", "tensor"), None, None)
    cache = P("dp", None, "tensor", None)
    heads = P("dp", None, None)
    return jax.shard_map(
        shards,
        mesh=mesh,
        in_specs=(
            heads, heads, heads, cache, cache, P("dp"), rows, P(), P(),
            P("tensor", None), P(), rows, rows, experts, experts, experts,
        ),
        out_specs=rows,
        check_vma=False,
    )
```

```python
import jax
import jax.numpy as jnp
from jax import lax
from jax.experimental import pallas as pl
from jax.experimental.pallas import tpu as pltpu
from jax.sharding import PartitionSpec as P

MESH = pl.DeviceIdType.MESH
F32 = jnp.float32
BF16 = jnp.bfloat16
VMEM = pltpu.VMEM

D = 4096
HALF = 2048
FFW = 768
SLOTS = 96
EPS = 1e-6
LOW = -1e30
ORDER = (("x", "y", "z"), ("y", "z", "x"), ("z", "x", "y"))
WAVES = (
    ((2, 0, 256), (0, 256, 256), (1, 512, 256)),
    ((2, 768, 512), (0, 1280, 384), (1, 1664, 384)),
)
PARTS = tuple(part for wave in WAVES for part in wave)
FORTH = ((0, 1, 2), (3, 4, 5))
BACK = ((0, 1, 2), (3, 4, 5))


def iota(shape, dim):
    return lax.broadcasted_iota(jnp.int32, shape, dim)


def dot(a, b):
    return jnp.dot(a, b, preferred_element_type=F32)


def kernel(
    q_hbm, nk_hbm, nv_hbm, kc_hbm, vc_hbm, len_hbm, res_hbm, qg_hbm, kg_hbm, ng_hbm, ids_hbm, gw_hbm,
    wp_hbm, wg_hbm, wu_hbm, wd_hbm,
    out_ref,
    q_ref, nk_ref, nv_ref, kc_ref, vc_ref, len_ref, res_ref, qg_ref, kg_ref, ng_ref, ids_ref, gw_ref,
    wp, wg, wu, wd,
    num_f, num_b, stat, stat_t, coef, rec_num, rec_stat, attn,
    pair_s, pair_r, send_b, rec_b, hidden, sq_own, sq_rec,
    table_s, table_r, packed, meta, plane_meta, disp, comb,
    x_full, perm, perm_t, acc, act, act_p,
    g, xs, xr, ys, yr, ps, rb, ra_s, ra_r,
    fin_s, fin_r,
    in_sem, w_sem, loc_sem, send_sem, recv_sem,
):
    dp = lax.axis_index("dp")
    t = lax.axis_index("tensor")
    here = {"z": dp // 4, "x": dp % 4, "y": t // 2, "c": t % 2}
    c = here["c"]

    def device(**moved):
        at = dict(here, **moved)
        return (at["z"] * 4 + at["x"], at["y"] * 2 + at["c"])

    def along(axis, k):
        return (here[axis] + k) % 4

    def tensor_peer(k):
        return (dp, (t + k) % 8)

    counter = [0]
    groups = []

    class Group:
        def __init__(self, like):
            self.index = counter[0]
            counter[0] += 1
            self.like = like
            groups.append(self)

        def copy(self, src, dst, to):
            return pltpu.make_async_remote_copy(
                src_ref=src,
                dst_ref=dst,
                send_sem=send_sem.at[self.index],
                recv_sem=recv_sem.at[self.index],
                device_id=to,
                device_id_type=MESH,
            )

        def send(self, src, dst, to):
            self.copy(src, dst, to).start()

        def wait_recv(self):
            self.copy(self.like, self.like, sibling).wait_recv()

        def wait_send(self):
            self.copy(self.like, self.like, sibling).wait_send()

    def remote(src, dst, to):
        group = Group(src)
        group.send(src, dst, to)
        return group

    sibling = device(c=1 - c)
    own_rows = pl.ds(pl.multiple_of(c * 8, 8), 8)
    other_rows = pl.ds(pl.multiple_of((1 - c) * 8, 8), 8)
    own_cols = pl.ds(pl.multiple_of(c * HALF, HALF), HALF)
    other_cols = pl.ds(pl.multiple_of((1 - c) * HALF, HALF), HALF)

    barrier = pltpu.get_barrier_semaphore()
    peers = [tensor_peer(k) for k in range(1, 8)]
    for axis in ("x", "z"):
        for k in (1, 2, 3):
            for core in (0, 1):
                peers.append(device(**{axis: along(axis, k), "c": core}))
    for peer in peers:
        pl.semaphore_signal(barrier, inc=1, device_id=peer, device_id_type=MESH)

    inputs = []
    for i, (src, dst) in enumerate(
        (
            (q_hbm, q_ref), (kc_hbm, kc_ref), (vc_hbm, vc_ref), (nk_hbm, nk_ref), (nv_hbm, nv_ref),
            (len_hbm, len_ref), (qg_hbm, qg_ref), (kg_hbm, kg_ref), (ids_hbm, ids_ref),
            (gw_hbm, gw_ref), (res_hbm, res_ref), (ng_hbm, ng_ref),
        )
    ):
        inputs.append(pltpu.make_async_copy(src, dst, in_sem.at[i]))
        inputs[-1].start()
    scaling = 128.0**-0.5
    first = (t == 0).astype(F32)
    shuffle = (iota((128, 128), 1) == (iota((128, 128), 0) % 8) * 16 + iota((128, 128), 0) // 8)
    shuffle = shuffle.astype(F32).astype(BF16)
    lane_row = iota((1, 256), 1) // 32
    lane_pos = iota((1, 256), 1) % 32 + t * 32
    own_block = (iota((128, 256), 0) % 8) == (iota((128, 256), 1) // 32)
    ones = jnp.ones((256, 128), BF16)
    lane = iota((8, 128), 1)
    stat[...] = jnp.zeros_like(stat)

    shares_a = Group(rec_num.at[pl.ds(1, 7)])

    def send_chunk(chunk):
        for k in (4, 3, 5, 2, 6, 1, 7):
            to = (t + k) % 8
            shares_a.send(num_b.at[chunk, pl.ds(to * 4, 4)], rec_num.at[k, chunk], (dp, to))

    def attend(blk, lower):
        at = pl.multiple_of(blk * 8, 8)
        rows = pl.ds(at, 8)
        limit = jnp.zeros((1, 256), jnp.int32)
        for r in range(8):
            limit = jnp.where(lane_row == r, len_ref[at + r], limit)
        bias = jnp.where(lane_pos < limit, 0.0, LOW)
        stats = jnp.zeros((8, 128), F32)
        for kv in range(2):
            q = q_ref[rows, pl.ds(kv * 16, 16), :].astype(F32).reshape(128, 128)
            q = q * lax.rsqrt(jnp.mean(q * q, axis=1, keepdims=True) + EPS) * qg_ref[...]
            q = dot(shuffle, q.astype(BF16)).astype(BF16)
            nk = nk_ref[rows, kv, :].astype(F32)
            nk = nk * lax.rsqrt(jnp.mean(nk * nk, axis=1, keepdims=True) + EPS) * kg_ref[...]
            nk = nk.astype(BF16).astype(F32)
            nv = nv_ref[rows, kv, :].astype(F32)
            keys = kc_ref[rows, kv].reshape(256, 128)
            values = vc_ref[rows, kv].reshape(256, 128)
            score = lax.dot_general(
                q, keys, (((1,), (1,)), ((), ())), preferred_element_type=F32
            )
            score = jnp.where(own_block, score * scaling + bias, LOW)
            fresh = (q.astype(F32).reshape(16, 8, 128) * nk[None]).reshape(128, 128)
            fresh = jnp.sum(fresh, axis=1, keepdims=True) * scaling
            top = jnp.maximum(jnp.max(score, axis=1, keepdims=True), fresh)
            weight = jnp.exp(score - top).astype(BF16)
            new_weight = jnp.exp(fresh - top).astype(BF16).astype(F32) * first
            number = dot(weight, values)
            total = dot(weight, ones) + new_weight
            number = number.reshape(16, 8, 128) + new_weight.reshape(16, 8, 1) * nv[None]
            top = jnp.broadcast_to(top, (128, 128)).reshape(16, 8, 128)
            total = total.reshape(16, 8, 128)
            for i in range(16):
                head = kv * 16 + i
                num_f[head, lower : lower + 8, :] = number[i]
                column = 8 * (head // 4) + head % 4
                stats = jnp.where(lane == column, top[i], stats)
                stats = jnp.where(lane == column + 4, total[i], stats)
        stat[rows, :] = stats

    def attend_chunk(chunk):
        attend(chunk * 2, 0)
        attend(chunk * 2 + 1, 8)
        num_b[chunk] = num_f[...].astype(BF16)

    for copy in inputs[:8]:
        copy.wait()
    weights = [pltpu.make_async_copy(wp_hbm, wp, w_sem.at[0])]
    weights[0].start()
    early = 2

    def attend_early(chunk, carry):
        attend_chunk(chunk)
        return carry

    lax.fori_loop(0, early, attend_early, 0)
    pl.semaphore_wait(barrier, len(peers))
    for chunk in range(early):
        send_chunk(chunk)

    for copy in inputs[8:]:
        copy.wait()
    gw = gw_ref[...]
    route = (gw / jnp.sum(gw, axis=1, keepdims=True)).astype(BF16)
    put = iota((8, 128), 1) - iota((8, 128), 0) - t * 16
    ids = ids_ref[...].astype(F32).astype(BF16)
    table = dot(ids, (put == 0).astype(F32).astype(BF16)) + dot(
        route, (put == 8).astype(F32).astype(BF16)
    )
    z, x, y = here["z"], here["x"], here["y"]
    table_s[...] = table
    spread = Group(table_r.at[pl.ds(1, 7)])
    for k in range(1, 8):
        spread.send(table_s, table_r.at[k], tensor_peer(k))

    hidden[own_rows, :] = res_ref[:, own_cols].astype(F32)
    fin_s[0] = res_ref[:, other_cols].astype(F32)
    res_copy = remote(fin_s.at[0], hidden.at[own_rows, :], sibling)

    def attend_more(chunk, carry):
        attend_chunk(chunk)
        send_chunk(chunk)
        return carry

    lax.fori_loop(early, 4, attend_more, 0)
    stat_t[...] = stat[...].T
    tops_a = Group(rec_stat.at[pl.ds(1, 7)])
    for k in (4, 3, 5, 2, 6, 1, 7):
        to = (t + k) % 8
        tile = pl.ds(pl.multiple_of(to * 8, 8), 8)
        tops_a.send(stat_t.at[tile, :], rec_stat.at[k], (dp, to))

    spread.wait_recv()
    table = table_s[...]
    for k in range(1, 8):
        table = table + table_r[k]
    packed[z, x] = table
    spread = Group(packed.at[z, pl.ds(0, 3)])
    for k in (1, 2, 3):
        spread.send(packed.at[z, x], packed.at[z, x], device(x=along("x", k)))
    for chunk in range(4):
        rec_num[0, chunk] = num_b[chunk, pl.ds(t * 4, 4)]
    rec_stat[0] = stat_t[pl.ds(pl.multiple_of(t * 8, 8), 8), :]
    for i, (src, dst) in enumerate(((wg_hbm, wg), (wu_hbm, wu), (wd_hbm, wd))):
        weights.append(pltpu.make_async_copy(src.at[0], dst, w_sem.at[1 + i]))
        weights[-1].start()
    row = iota((384, 384), 0)
    col = iota((384, 384), 1)
    zz, yy, xx, rest = row // 96, (row // 24) % 4, (row // 6) % 4, row % 6
    perm[0] = (col == xx * 96 + zz * 24 + yy * 6 + rest).astype(F32).astype(BF16)
    perm[1] = (col == yy * 96 + xx * 24 + zz * 6 + rest).astype(F32).astype(BF16)
    zz, yy, xx, rest = col // 96, (col // 24) % 4, (col // 6) % 4, col % 6
    perm_t[0] = (row == xx * 96 + zz * 24 + yy * 6 + rest).astype(F32).astype(BF16)
    perm_t[1] = (row == yy * 96 + xx * 24 + zz * 6 + rest).astype(F32).astype(BF16)

    tops_a.wait_recv()
    shares_a.wait_recv()
    spread.wait_recv()
    spread = Group(packed.at[pl.ds(0, 3)])
    for k in (1, 2, 3):
        spread.send(packed.at[z], packed.at[z], device(z=along("z", k)))
    tops = [rec_stat[k][0:4] for k in range(8)]
    best = tops[0]
    for top in tops[1:]:
        best = jnp.maximum(best, top)
    scale = [jnp.exp(top - best) for top in tops]
    whole = scale[0] * rec_stat[0][4:8]
    for k in range(1, 8):
        whole = whole + scale[k] * rec_stat[k][4:8]
    coef[...] = jnp.zeros_like(coef)
    for k in range(8):
        coef[8 * k : 8 * k + 4, :] = scale[k] / whole
    columns = coef[...].T
    for j in range(4):
        out = jnp.zeros((64, 128), F32)
        for k in range(8):
            out = out + columns[0:64, 8 * k + j : 8 * k + j + 1] * rec_num[k, :, j].reshape(64, 128).astype(F32)
        attn[:, 128 * j : 128 * j + 128] = out.astype(BF16)

    weights[0].wait()
    pairs = []
    for j in (0, 1):
        for tile in (0, 1):
            cols = pl.ds(pl.multiple_of((1 - c) * HALF + j * 1024 + tile * 512, 512), 512)
            pair_s[j, :, tile * 512 : tile * 512 + 512] = dot(attn[...], wp[:, cols]).astype(BF16)
        pairs.append(remote(pair_s.at[j], pair_r.at[j], sibling))
    shares = Group(rec_b.at[pl.ds(1, 3)])
    for j in (0, 1):
        for tile in (0, 1):
            cols = pl.ds(pl.multiple_of(c * HALF + j * 1024 + tile * 512, 512), 512)
            part = dot(attn[...], wp[:, cols])
            if tile == 0:
                pairs[j].wait_recv()
            at = slice(tile * 512, tile * 512 + 512)
            send_b[j, :, at] = (part + pair_r[j, :, at].astype(F32)).astype(BF16)
        for k in (2, 1, 3):
            to = along("y", k)
            rows = pl.ds(pl.multiple_of(to * 16, 16), 16)
            shares.send(send_b.at[j, rows, :], rec_b.at[k, j], device(y=to))

    spread.wait_recv()
    for tile in range(8):
        for iz in range(4):
            for ix in range(4):
                rows8 = packed[iz, ix]
                if tile > 0:
                    rows8 = pltpu.roll(rows8, 128 - 16 * tile, 1)
                meta[iz, ix, tile // 2, tile % 2] = rows8
    before = iota((256, 256), 0)
    after = iota((256, 256), 1)
    earlier = ((before // 8 == after // 8) & (before < after)).astype(F32).astype(BF16)
    slot_base = ((iota((1, 256), 1) // 8) * 3).astype(F32)
    slot_id = iota((SLOTS, 256), 0).astype(F32)
    for p in range(3):
        a, b, last = ORDER[p]
        for ib in range(4):
            for ia in range(4):
                at = dict(here, **{a: ia, b: ib})
                plane_meta[pl.ds((ib * 4 + ia) * 16, 16), :] = meta[
                    at["z"], at["x"], at["y"]
                ].reshape(16, 128)
        table = plane_meta[...].T
        chosen, gates = table[0:8], table[8:16]
        for k in range(4):
            for core in range(2):
                at = dict(here, **{last: k, "c": core})
                expert = (at["z"] * 32 + at["x"] * 8 + at["y"] * 2 + at["c"]).astype(F32)
                hit = (chosen == expert).astype(F32)
                used = jnp.sum(hit, axis=0, keepdims=True)
                gate = jnp.sum(hit * gates, axis=0, keepdims=True)
                rank = dot(jnp.broadcast_to(used, (8, 256)).astype(BF16), earlier)[0:1]
                slot = jnp.where(used > 0.5, slot_base + rank, -1.0)
                match = slot == slot_id
                first_slot = (k * 2 + core) * SLOTS
                disp[p, first_slot : first_slot + SLOTS, :] = match.astype(F32).astype(BF16)
                comb[p, first_slot : first_slot + SLOTS, :] = jnp.where(match, gate, 0.0).astype(BF16)

    res_copy.wait_recv()
    shares.wait_recv()
    rows = pl.ds(pl.multiple_of(y * 16, 16), 16)
    for j in (0, 1):
        total = send_b[j, rows, :].astype(F32)
        for k in (1, 2, 3):
            total = total + rec_b[k, j].astype(F32)
        at = slice(j * 1024, j * 1024 + 1024)
        hidden[:, at] = hidden[:, at] + total
    value = hidden[...]
    squares = jnp.sum(value * value, axis=1, keepdims=True)
    sq_own[...] = jnp.broadcast_to(squares, (16, 128))
    sq_copy = remote(sq_own, sq_rec, sibling)
    sq_copy.wait_recv()
    mean = (squares + sq_rec[:, 0:1]) * (1.0 / D)
    normed = (value * lax.rsqrt(mean + EPS) * ng_ref[:, own_cols]).astype(BF16)

    stage = {}
    for wave in FORTH:
        for p in wave:
            order, first, width = PARTS[p]
            a, b, last = ORDER[order]
            g[p][here[b], here[a]] = normed[:, first : first + width]
            unit = g[p].at[here[b], here[a]]
            stage[p] = Group(g[p].at[here[b], pl.ds(0, 3)])
            for k in (2, 1, 3):
                stage[p].send(unit, unit, device(**{a: along(a, k)}))
    for wave in FORTH:
        for p in wave:
            a, b, last = ORDER[PARTS[p][0]]
            stage[p].wait_recv()
            unit = g[p].at[here[b]]
            stage[p] = Group(g[p].at[pl.ds(0, 3)])
            for k in (2, 1, 3):
                stage[p].send(unit, unit, device(**{b: along(b, k)}))
    locals_in = {}
    for wave in FORTH:
        for p in wave:
            order, first, width = PARTS[p]
            a, b, last = ORDER[order]
            stage[p].wait_recv()
            plane = g[p][...].reshape(256, width)
            stage[p] = Group(xs[p].at[pl.ds(0, 7)])
            for k in (2, 1, 3, 0):
                to = along(last, k)
                wanted = pl.ds(pl.multiple_of(to * 2 * SLOTS, 2 * SLOTS), 2 * SLOTS)
                picked = dot(disp[order, wanted, :], plane)
                xs[p][2 * k : 2 * k + 2] = picked.astype(BF16).reshape(2, SLOTS, width)
                for j in (1, 0):
                    core = (c + j) % 2
                    src = xs[p].at[2 * k + core]
                    dst = xr[p].at[c, here[last]]
                    if k == 0 and j == 0:
                        local = pltpu.make_async_copy(src, dst, loc_sem.at[p])
                        local.start()
                        locals_in[p] = local
                    else:
                        stage[p].send(src, dst, device(**{last: to, "c": core}))
    for n, wave in enumerate(FORTH):
        for p in wave:
            order, first, width = PARTS[p]
            stage[p].wait_recv()
            locals_in[p].wait()
            for half in (0, 1):
                block = xr[p][half].reshape(384, width)
                if order > 0:
                    block = dot(perm[order - 1], block).astype(BF16)
                x_full[:, half * HALF + first : half * HALF + first + width] = block
        if n == 0:
            for copy in weights[1:]:
                copy.wait()
        low = min(PARTS[p][1] for p in wave)
        high = max(PARTS[p][1] + PARTS[p][2] for p in wave)

        def expert(i, carry, n=n, low=low, high=high):
            cols = pl.ds(pl.multiple_of(i * 256, 256), 256)
            sums = []
            for which, weight in ((0, wg), (1, wu)):
                total = dot(x_full[:, low:high], weight[low:high, cols])
                total = total + dot(
                    x_full[:, HALF + low : HALF + high], weight[HALF + low : HALF + high, cols]
                )
                if n > 0:
                    total = total + acc[which, :, cols]
                if n < len(FORTH) - 1:
                    acc[which, :, cols] = total
                sums.append(total)
            if n == len(FORTH) - 1:
                gate, up = sums
                act[:, cols] = (gate / (1.0 + jnp.exp(-gate)) * up).astype(BF16)
            return carry

        lax.fori_loop(0, FFW // 256, expert, 0)

    stage, locals_out, ready = {}, {}, []
    for wave in BACK:
        for p in wave:
            order, first, width = PARTS[p]
            a, b, last = ORDER[order]
            if order == 0:
                turned = act
            else:
                turned = act_p.at[order - 1]
                if order not in ready:
                    ready.append(order)
                    turned[...] = dot(perm_t[order - 1], act[...]).astype(BF16)
            stage[p] = Group(ys[p].at[pl.ds(0, 7)])
            for j in (1, 0):
                core = (c + j) % 2
                cols = pl.ds(pl.multiple_of(core * HALF + first, 128), width)
                result = dot(turned[...], wd[:, cols])
                ys[p][4 * j : 4 * j + 4] = result.astype(BF16).reshape(4, SLOTS, width)
                for k in (2, 1, 3, 0):
                    to = along(last, k)
                    src = ys[p].at[4 * j + to]
                    dst = yr[p].at[here[last] * 2 + c]
                    if k == 0 and j == 0:
                        local = pltpu.make_async_copy(src, dst, loc_sem.at[len(PARTS) + p])
                        local.start()
                        locals_out[p] = local
                    else:
                        stage[p].send(src, dst, device(**{last: to, "c": core}))
    for wave in BACK:
        for p in wave:
            order, first, width = PARTS[p]
            a, b, last = ORDER[order]
            stage[p].wait_recv()
            locals_out[p].wait()
            summed = lax.dot_general(
                comb[order], yr[p][...].reshape(8 * SLOTS, width), (((0,), (0,)), ((), ())),
                preferred_element_type=F32,
            )
            ps[p][...] = summed.astype(BF16).reshape(4, 64, width)
            stage[p] = Group(ps[p].at[pl.ds(0, 3)])
            for k in (2, 1, 3):
                to = along(b, k)
                stage[p].send(ps[p].at[to], rb[p].at[k], device(**{b: to}))
        for p in wave:
            order, first, width = PARTS[p]
            a, b, last = ORDER[order]
            stage[p].wait_recv()
            total = ps[p][here[b]].astype(F32)
            for k in (1, 2, 3):
                total = total + rb[p][k].astype(F32)
            ra_s[p][...] = total.astype(BF16).reshape(4, 16, width)
            stage[p] = Group(ra_s[p].at[pl.ds(0, 3)])
            for k in (2, 1, 3):
                to = along(a, k)
                stage[p].send(ra_s[p].at[to], ra_r[p].at[k], device(**{a: to}))
    for wave in BACK:
        for p in wave:
            order, first, width = PARTS[p]
            a, b, last = ORDER[order]
            stage[p].wait_recv()
            total = ra_s[p][here[a]].astype(F32)
            for k in (1, 2, 3):
                total = total + ra_r[p][k].astype(F32)
            cols = slice(first, first + width)
            hidden[:, cols] = hidden[:, cols] + total

    fin_s[1] = hidden[other_rows, :]
    fin = remote(fin_s.at[1], fin_r, sibling)
    out_ref[:, own_cols] = hidden[own_rows, :].astype(BF16)
    fin.wait_recv()
    out_ref[:, other_cols] = fin_r[...].astype(BF16)
    for group in groups:
        group.wait_send()


GROUPS = 11 + 6 * len(PARTS)


def shards(
    queries, new_keys, new_values, key_cache, value_cache, lengths, residual_in, query_gain, key_gain,
    out_proj, norm_gain, expert_ids, gate_weights, expert_gate, expert_up, expert_down,
):
    anywhere = pl.BlockSpec(memory_space=pl.ANY)

    def each(shape_of):
        return [VMEM(shape_of(width), BF16) for _, _, width in PARTS]

    return pl.pallas_call(
        kernel,
        out_shape=jax.ShapeDtypeStruct((8, D), BF16),
        in_specs=[anywhere] * 16,
        out_specs=pl.BlockSpec(memory_space=pltpu.VMEM),
        scratch_shapes=[
            VMEM((64, 32, 128), BF16), VMEM((64, 2, 128), BF16), VMEM((64, 2, 128), BF16),
            VMEM((64, 2, 32, 128), BF16), VMEM((64, 2, 32, 128), BF16), pltpu.SMEM((64,), jnp.int32),
            VMEM((8, D), BF16), VMEM((1, 128), F32), VMEM((1, 128), F32), VMEM((1, D), F32),
            VMEM((8, 8), jnp.int32), VMEM((8, 8), F32),
            VMEM((512, D), BF16), VMEM((D, FFW), BF16), VMEM((D, FFW), BF16), VMEM((FFW, D), BF16),
            VMEM((32, 16, 128), F32), VMEM((4, 32, 16, 128), BF16), VMEM((128, 128), F32),
            VMEM((128, 128), F32), VMEM((128, 128), F32), VMEM((8, 4, 4, 16, 128), BF16),
            VMEM((8, 8, 128), F32), VMEM((64, 512), BF16),
            VMEM((2, 64, 1024), BF16), VMEM((2, 64, 1024), BF16), VMEM((2, 64, 1024), BF16),
            VMEM((4, 2, 16, 1024), BF16), VMEM((16, HALF), F32),
            VMEM((16, 128), F32), VMEM((16, 128), F32),
            VMEM((8, 128), F32), VMEM((8, 8, 128), F32), VMEM((4, 4, 8, 128), F32),
            VMEM((4, 4, 4, 2, 8, 128), F32), VMEM((256, 128), F32),
            VMEM((3, 8 * SLOTS, 256), BF16), VMEM((3, 8 * SLOTS, 256), BF16),
            VMEM((384, D), BF16), VMEM((2, 384, 384), BF16), VMEM((2, 384, 384), BF16),
            VMEM((2, 384, FFW), F32), VMEM((384, FFW), BF16), VMEM((2, 384, FFW), BF16),
            each(lambda w: (4, 4, 16, w)),
            each(lambda w: (8, SLOTS, w)),
            each(lambda w: (2, 4, SLOTS, w)),
            each(lambda w: (8, SLOTS, w)),
            each(lambda w: (8, SLOTS, w)),
            each(lambda w: (4, 64, w)), each(lambda w: (4, 64, w)),
            each(lambda w: (4, 16, w)), each(lambda w: (4, 16, w)),
            VMEM((2, 8, HALF), F32), VMEM((8, HALF), F32),
            pltpu.SemaphoreType.DMA((12,)), pltpu.SemaphoreType.DMA((4,)), pltpu.SemaphoreType.DMA((2 * len(PARTS),)),
            pltpu.SemaphoreType.DMA((GROUPS,)), pltpu.SemaphoreType.DMA((GROUPS,)),
        ],
        compiler_params=pltpu.CompilerParams(
            collective_id=0, has_side_effects=True, vmem_limit_bytes=60 * 2**20
        ),
        cost_estimate=pl.CostEstimate(flops=10**10, bytes_accessed=26 * 2**20, transcendentals=10**6),
    )(
        queries, new_keys, new_values, key_cache, value_cache, lengths, residual_in,
        query_gain.reshape(1, 128), key_gain.reshape(1, 128), norm_gain.reshape(1, D),
        expert_ids, gate_weights, out_proj, expert_gate, expert_up, expert_down,
    )


def solution(mesh):
    rows = P(("dp", "tensor"), None)
    experts = P(("dp", "tensor"), None, None)
    cache = P("dp", None, "tensor", None)
    heads = P("dp", None, None)
    return jax.shard_map(
        shards,
        mesh=mesh,
        in_specs=(
            heads, heads, heads, cache, cache, P("dp"), rows, P(), P(),
            P("tensor", None), P(), rows, rows, experts, experts, experts,
        ),
        out_specs=rows,
        check_vma=False,
    )
```

```python
import jax
import jax.numpy as jnp
from jax import lax
from jax.experimental import pallas as pl
from jax.experimental.pallas import tpu as pltpu
from jax.sharding import PartitionSpec as P

MESH = pl.DeviceIdType.MESH
F32 = jnp.float32
BF16 = jnp.bfloat16
VMEM = pltpu.VMEM

D = 4096
HALF = 2048
FFW = 768
SLOTS = 96
EPS = 1e-6
LOW = -1e30
ORDER = (("x", "y", "z"), ("y", "z", "x"), ("z", "x", "y"))
WAVES = (
    ((2, 0, 256), (0, 256, 256), (1, 512, 256)),
    ((2, 768, 512), (0, 1280, 384), (1, 1664, 384)),
)
PARTS = tuple(part for wave in WAVES for part in wave)
FORTH = ((0, 1, 2), (3, 4, 5))
BACK = ((0, 1, 2), (3, 4, 5))


def iota(shape, dim):
    return lax.broadcasted_iota(jnp.int32, shape, dim)


def dot(a, b):
    return jnp.dot(a, b, preferred_element_type=F32)


def kernel(
    q_hbm, nk_hbm, nv_hbm, kc_hbm, vc_hbm, len_hbm, res_hbm, qg_hbm, kg_hbm, ng_hbm, ids_hbm, gw_hbm,
    wp_hbm, wg_hbm, wu_hbm, wd_hbm,
    out_ref,
    q_ref, nk_ref, nv_ref, kc_ref, vc_ref, len_ref, res_ref, qg_ref, kg_ref, ng_ref, ids_ref, gw_ref,
    wp, wg, wu, wd,
    q_n, q_s, num_f, num_b, stat, stat_t, coef, rec_num, rec_stat, attn,
    pair_s, pair_r, send_b, rec_b, hidden, sq_own, sq_rec,
    table_s, table_r, packed, meta, plane_meta, disp, comb,
    x_full, perm, perm_t, acc, act, act_p,
    g, xs, xr, ys, yr, ps, rb, ra_s, ra_r,
    fin_s, fin_r,
    in_sem, w_sem, loc_sem, send_sem, recv_sem,
):
    dp = lax.axis_index("dp")
    t = lax.axis_index("tensor")
    here = {"z": dp // 4, "x": dp % 4, "y": t // 2, "c": t % 2}
    c = here["c"]

    def device(**moved):
        at = dict(here, **moved)
        return (at["z"] * 4 + at["x"], at["y"] * 2 + at["c"])

    def along(axis, k):
        return (here[axis] + k) % 4

    def tensor_peer(k):
        return (dp, (t + k) % 8)

    counter = [0]
    groups = []

    class Group:
        def __init__(self, like):
            self.index = counter[0]
            counter[0] += 1
            self.like = like
            groups.append(self)

        def copy(self, src, dst, to):
            return pltpu.make_async_remote_copy(
                src_ref=src,
                dst_ref=dst,
                send_sem=send_sem.at[self.index],
                recv_sem=recv_sem.at[self.index],
                device_id=to,
                device_id_type=MESH,
            )

        def send(self, src, dst, to):
            self.copy(src, dst, to).start()

        def wait_recv(self):
            self.copy(self.like, self.like, sibling).wait_recv()

        def wait_send(self):
            self.copy(self.like, self.like, sibling).wait_send()

    def remote(src, dst, to):
        group = Group(src)
        group.send(src, dst, to)
        return group

    sibling = device(c=1 - c)
    own_rows = pl.ds(pl.multiple_of(c * 8, 8), 8)
    other_rows = pl.ds(pl.multiple_of((1 - c) * 8, 8), 8)
    own_cols = pl.ds(pl.multiple_of(c * HALF, HALF), HALF)
    other_cols = pl.ds(pl.multiple_of((1 - c) * HALF, HALF), HALF)

    barrier = pltpu.get_barrier_semaphore()
    peers = [tensor_peer(k) for k in range(1, 8)]
    for axis in ("x", "z"):
        for k in (1, 2, 3):
            for core in (0, 1):
                peers.append(device(**{axis: along(axis, k), "c": core}))
    for peer in peers:
        pl.semaphore_signal(barrier, inc=1, device_id=peer, device_id_type=MESH)

    inputs = []
    for i, (src, dst) in enumerate(
        (
            (q_hbm, q_ref), (kc_hbm, kc_ref), (vc_hbm, vc_ref), (nk_hbm, nk_ref), (nv_hbm, nv_ref),
            (len_hbm, len_ref), (qg_hbm, qg_ref), (kg_hbm, kg_ref), (ids_hbm, ids_ref),
            (gw_hbm, gw_ref), (res_hbm, res_ref), (ng_hbm, ng_ref),
        )
    ):
        inputs.append(pltpu.make_async_copy(src, dst, in_sem.at[i]))
        inputs[-1].start()
    scaling = 128.0**-0.5
    first = (t == 0).astype(F32)
    shuffle = (iota((128, 128), 1) == (iota((128, 128), 0) % 8) * 16 + iota((128, 128), 0) // 8)
    shuffle = shuffle.astype(F32).astype(BF16)
    lane_row = iota((1, 256), 1) // 32
    lane_pos = iota((1, 256), 1) % 32 + t * 32
    own_block = (iota((128, 256), 0) % 8) == (iota((128, 256), 1) // 32)
    ones = jnp.ones((256, 128), BF16)
    lane = iota((8, 128), 1)
    stat[...] = jnp.zeros_like(stat)

    shares_a = Group(rec_num.at[pl.ds(1, 7)])

    def send_chunk(chunk):
        for k in (4, 3, 5, 2, 6, 1, 7):
            to = (t + k) % 8
            shares_a.send(num_b.at[chunk, pl.ds(to * 4, 4)], rec_num.at[k, chunk], (dp, to))

    def attend(blk, lower):
        at = pl.multiple_of(blk * 8, 8)
        rows = pl.ds(at, 8)
        limit = jnp.zeros((1, 256), jnp.int32)
        for r in range(8):
            limit = jnp.where(lane_row == r, len_ref[at + r], limit)
        bias = jnp.where(lane_pos < limit, 0.0, LOW)
        stats = jnp.zeros((8, 128), F32)
        for kv in range(2):
            place = (lower // 8) * 2 + kv
            q = q_s[:, place * 128 : place * 128 + 128]
            nk = nk_ref[rows, kv, :].astype(F32)
            nk = nk * lax.rsqrt(jnp.mean(nk * nk, axis=1, keepdims=True) + EPS) * kg_ref[...]
            nk = nk.astype(BF16).astype(F32)
            nv = nv_ref[rows, kv, :].astype(F32)
            keys = kc_ref[rows, kv].reshape(256, 128)
            values = vc_ref[rows, kv].reshape(256, 128)
            score = lax.dot_general(
                q, keys, (((1,), (1,)), ((), ())), preferred_element_type=F32
            )
            score = jnp.where(own_block, score * scaling + bias, LOW)
            fresh = (q.astype(F32).reshape(16, 8, 128) * nk[None]).reshape(128, 128)
            fresh = jnp.sum(fresh, axis=1, keepdims=True) * scaling
            top = jnp.maximum(jnp.max(score, axis=1, keepdims=True), fresh)
            weight = jnp.exp(score - top).astype(BF16)
            new_weight = jnp.exp(fresh - top).astype(BF16).astype(F32) * first
            number = dot(weight, values)
            total = dot(weight, ones) + new_weight
            number = number.reshape(16, 8, 128) + new_weight.reshape(16, 8, 1) * nv[None]
            top = jnp.broadcast_to(top, (128, 128)).reshape(16, 8, 128)
            total = total.reshape(16, 8, 128)
            for i in range(16):
                head = kv * 16 + i
                num_f[head, lower : lower + 8, :] = number[i]
                column = 8 * (head // 4) + head % 4
                stats = jnp.where(lane == column, top[i], stats)
                stats = jnp.where(lane == column + 4, total[i], stats)
        stat[rows, :] = stats

    def attend_chunk(chunk):
        for sub in (0, 1):
            rows = pl.ds(pl.multiple_of(chunk * 16 + sub * 8, 8), 8)
            for kv in (0, 1):
                q = q_ref[rows, pl.ds(kv * 16, 16), :].astype(F32).reshape(128, 128)
                q = q * lax.rsqrt(jnp.mean(q * q, axis=1, keepdims=True) + EPS) * qg_ref[...]
                place = sub * 2 + kv
                q_n[:, place * 128 : place * 128 + 128] = q.astype(BF16)
        q_s[...] = dot(shuffle, q_n[...]).astype(BF16)
        attend(chunk * 2, 0)
        attend(chunk * 2 + 1, 8)
        num_b[chunk] = num_f[...].astype(BF16)

    for copy in inputs[:8]:
        copy.wait()
    weights = [pltpu.make_async_copy(wp_hbm, wp, w_sem.at[0])]
    weights[0].start()
    attend_chunk(0)
    pl.semaphore_wait(barrier, len(peers))
    send_chunk(0)

    for copy in inputs[8:]:
        copy.wait()
    gw = gw_ref[...]
    route = (gw / jnp.sum(gw, axis=1, keepdims=True)).astype(BF16)
    put = iota((8, 128), 1) - iota((8, 128), 0) - t * 16
    ids = ids_ref[...].astype(F32).astype(BF16)
    table = dot(ids, (put == 0).astype(F32).astype(BF16)) + dot(
        route, (put == 8).astype(F32).astype(BF16)
    )
    z, x, y = here["z"], here["x"], here["y"]
    table_s[...] = table
    spread = Group(table_r.at[pl.ds(1, 7)])
    for k in range(1, 8):
        spread.send(table_s, table_r.at[k], tensor_peer(k))

    hidden[own_rows, :] = res_ref[:, own_cols].astype(F32)
    fin_s[0] = res_ref[:, other_cols].astype(F32)
    res_copy = remote(fin_s.at[0], hidden.at[own_rows, :], sibling)

    def attend_more(chunk, carry):
        attend_chunk(chunk)
        send_chunk(chunk)
        return carry

    lax.fori_loop(1, 4, attend_more, 0)
    stat_t[...] = stat[...].T
    tops_a = Group(rec_stat.at[pl.ds(1, 7)])
    for k in (4, 3, 5, 2, 6, 1, 7):
        to = (t + k) % 8
        tile = pl.ds(pl.multiple_of(to * 8, 8), 8)
        tops_a.send(stat_t.at[tile, :], rec_stat.at[k], (dp, to))

    spread.wait_recv()
    table = table_s[...]
    for k in range(1, 8):
        table = table + table_r[k]
    packed[z, x] = table
    spread = Group(packed.at[z, pl.ds(0, 3)])
    for k in (1, 2, 3):
        spread.send(packed.at[z, x], packed.at[z, x], device(x=along("x", k)))
    for chunk in range(4):
        rec_num[0, chunk] = num_b[chunk, pl.ds(t * 4, 4)]
    rec_stat[0] = stat_t[pl.ds(pl.multiple_of(t * 8, 8), 8), :]
    for i, (src, dst) in enumerate(((wg_hbm, wg), (wu_hbm, wu), (wd_hbm, wd))):
        weights.append(pltpu.make_async_copy(src.at[0], dst, w_sem.at[1 + i]))
        weights[-1].start()
    row = iota((384, 384), 0)
    col = iota((384, 384), 1)
    zz, yy, xx, rest = row // 96, (row // 24) % 4, (row // 6) % 4, row % 6
    perm[0] = (col == xx * 96 + zz * 24 + yy * 6 + rest).astype(F32).astype(BF16)
    perm[1] = (col == yy * 96 + xx * 24 + zz * 6 + rest).astype(F32).astype(BF16)
    zz, yy, xx, rest = col // 96, (col // 24) % 4, (col // 6) % 4, col % 6
    perm_t[0] = (row == xx * 96 + zz * 24 + yy * 6 + rest).astype(F32).astype(BF16)
    perm_t[1] = (row == yy * 96 + xx * 24 + zz * 6 + rest).astype(F32).astype(BF16)

    tops_a.wait_recv()
    shares_a.wait_recv()
    spread.wait_recv()
    spread = Group(packed.at[pl.ds(0, 3)])
    for k in (1, 2, 3):
        spread.send(packed.at[z], packed.at[z], device(z=along("z", k)))
    tops = [rec_stat[k][0:4] for k in range(8)]
    best = tops[0]
    for top in tops[1:]:
        best = jnp.maximum(best, top)
    scale = [jnp.exp(top - best) for top in tops]
    whole = scale[0] * rec_stat[0][4:8]
    for k in range(1, 8):
        whole = whole + scale[k] * rec_stat[k][4:8]
    coef[...] = jnp.zeros_like(coef)
    for k in range(8):
        coef[8 * k : 8 * k + 4, :] = scale[k] / whole
    columns = coef[...].T
    for j in range(4):
        out = jnp.zeros((64, 128), F32)
        for k in range(8):
            out = out + columns[0:64, 8 * k + j : 8 * k + j + 1] * rec_num[k, :, j].reshape(64, 128).astype(F32)
        attn[:, 128 * j : 128 * j + 128] = out.astype(BF16)

    weights[0].wait()
    pairs = []
    for j in (0, 1):
        for tile in (0, 1):
            cols = pl.ds(pl.multiple_of((1 - c) * HALF + j * 1024 + tile * 512, 512), 512)
            pair_s[j, :, tile * 512 : tile * 512 + 512] = dot(attn[...], wp[:, cols]).astype(BF16)
        pairs.append(remote(pair_s.at[j], pair_r.at[j], sibling))
    shares = Group(rec_b.at[pl.ds(1, 3)])
    for j in (0, 1):
        for tile in (0, 1):
            cols = pl.ds(pl.multiple_of(c * HALF + j * 1024 + tile * 512, 512), 512)
            part = dot(attn[...], wp[:, cols])
            if tile == 0:
                pairs[j].wait_recv()
            at = slice(tile * 512, tile * 512 + 512)
            send_b[j, :, at] = (part + pair_r[j, :, at].astype(F32)).astype(BF16)
        for k in (2, 1, 3):
            to = along("y", k)
            rows = pl.ds(pl.multiple_of(to * 16, 16), 16)
            shares.send(send_b.at[j, rows, :], rec_b.at[k, j], device(y=to))

    spread.wait_recv()
    for tile in range(8):
        for iz in range(4):
            for ix in range(4):
                rows8 = packed[iz, ix]
                if tile > 0:
                    rows8 = pltpu.roll(rows8, 128 - 16 * tile, 1)
                meta[iz, ix, tile // 2, tile % 2] = rows8
    before = iota((256, 256), 0)
    after = iota((256, 256), 1)
    earlier = ((before // 8 == after // 8) & (before < after)).astype(F32).astype(BF16)
    slot_base = ((iota((1, 256), 1) // 8) * 3).astype(F32)
    slot_id = iota((SLOTS, 256), 0).astype(F32)
    for p in range(3):
        a, b, last = ORDER[p]
        for ib in range(4):
            for ia in range(4):
                at = dict(here, **{a: ia, b: ib})
                plane_meta[pl.ds((ib * 4 + ia) * 16, 16), :] = meta[
                    at["z"], at["x"], at["y"]
                ].reshape(16, 128)
        table = plane_meta[...].T
        chosen, gates = table[0:8], table[8:16]
        for k in range(4):
            for core in range(2):
                at = dict(here, **{last: k, "c": core})
                expert = (at["z"] * 32 + at["x"] * 8 + at["y"] * 2 + at["c"]).astype(F32)
                hit = (chosen == expert).astype(F32)
                used = jnp.sum(hit, axis=0, keepdims=True)
                gate = jnp.sum(hit * gates, axis=0, keepdims=True)
                rank = dot(jnp.broadcast_to(used, (8, 256)).astype(BF16), earlier)[0:1]
                slot = jnp.where(used > 0.5, slot_base + rank, -1.0)
                match = slot == slot_id
                first_slot = (k * 2 + core) * SLOTS
                disp[p, first_slot : first_slot + SLOTS, :] = match.astype(F32).astype(BF16)
                comb[p, first_slot : first_slot + SLOTS, :] = jnp.where(match, gate, 0.0).astype(BF16)

    res_copy.wait_recv()
    shares.wait_recv()
    rows = pl.ds(pl.multiple_of(y * 16, 16), 16)
    for j in (0, 1):
        total = send_b[j, rows, :].astype(F32)
        for k in (1, 2, 3):
            total = total + rec_b[k, j].astype(F32)
        at = slice(j * 1024, j * 1024 + 1024)
        hidden[:, at] = hidden[:, at] + total
    value = hidden[...]
    squares = jnp.sum(value * value, axis=1, keepdims=True)
    sq_own[...] = jnp.broadcast_to(squares, (16, 128))
    sq_copy = remote(sq_own, sq_rec, sibling)
    sq_copy.wait_recv()
    mean = (squares + sq_rec[:, 0:1]) * (1.0 / D)
    normed = (value * lax.rsqrt(mean + EPS) * ng_ref[:, own_cols]).astype(BF16)

    stage = {}
    for wave in FORTH:
        for p in wave:
            order, first, width = PARTS[p]
            a, b, last = ORDER[order]
            g[p][here[b], here[a]] = normed[:, first : first + width]
            unit = g[p].at[here[b], here[a]]
            stage[p] = Group(g[p].at[here[b], pl.ds(0, 3)])
            for k in (2, 1, 3):
                stage[p].send(unit, unit, device(**{a: along(a, k)}))
    for wave in FORTH:
        for p in wave:
            a, b, last = ORDER[PARTS[p][0]]
            stage[p].wait_recv()
            unit = g[p].at[here[b]]
            stage[p] = Group(g[p].at[pl.ds(0, 3)])
            for k in (2, 1, 3):
                stage[p].send(unit, unit, device(**{b: along(b, k)}))
    locals_in = {}
    for wave in FORTH:
        for p in wave:
            order, first, width = PARTS[p]
            a, b, last = ORDER[order]
            stage[p].wait_recv()
            plane = g[p][...].reshape(256, width)
            stage[p] = Group(xs[p].at[pl.ds(0, 7)])
            for k in (2, 1, 3, 0):
                to = along(last, k)
                wanted = pl.ds(pl.multiple_of(to * 2 * SLOTS, 2 * SLOTS), 2 * SLOTS)
                picked = dot(disp[order, wanted, :], plane)
                xs[p][2 * k : 2 * k + 2] = picked.astype(BF16).reshape(2, SLOTS, width)
                for j in (1, 0):
                    core = (c + j) % 2
                    src = xs[p].at[2 * k + core]
                    dst = xr[p].at[c, here[last]]
                    if k == 0 and j == 0:
                        local = pltpu.make_async_copy(src, dst, loc_sem.at[p])
                        local.start()
                        locals_in[p] = local
                    else:
                        stage[p].send(src, dst, device(**{last: to, "c": core}))
    for n, wave in enumerate(FORTH):
        for p in wave:
            order, first, width = PARTS[p]
            stage[p].wait_recv()
            locals_in[p].wait()
            for half in (0, 1):
                block = xr[p][half].reshape(384, width)
                if order > 0:
                    block = dot(perm[order - 1], block).astype(BF16)
                x_full[:, half * HALF + first : half * HALF + first + width] = block
        if n == 0:
            for copy in weights[1:]:
                copy.wait()
        low = min(PARTS[p][1] for p in wave)
        high = max(PARTS[p][1] + PARTS[p][2] for p in wave)

        def expert(i, carry, n=n, low=low, high=high):
            cols = pl.ds(pl.multiple_of(i * 256, 256), 256)
            sums = []
            for which, weight in ((0, wg), (1, wu)):
                total = dot(x_full[:, low:high], weight[low:high, cols])
                total = total + dot(
                    x_full[:, HALF + low : HALF + high], weight[HALF + low : HALF + high, cols]
                )
                if n > 0:
                    total = total + acc[which, :, cols]
                if n < len(FORTH) - 1:
                    acc[which, :, cols] = total
                sums.append(total)
            if n == len(FORTH) - 1:
                gate, up = sums
                act[:, cols] = (gate / (1.0 + jnp.exp(-gate)) * up).astype(BF16)
            return carry

        lax.fori_loop(0, FFW // 256, expert, 0)

    stage, locals_out, ready = {}, {}, []
    for wave in BACK:
        for p in wave:
            order, first, width = PARTS[p]
            a, b, last = ORDER[order]
            if order == 0:
                turned = act
            else:
                turned = act_p.at[order - 1]
                if order not in ready:
                    ready.append(order)
                    turned[...] = dot(perm_t[order - 1], act[...]).astype(BF16)
            stage[p] = Group(ys[p].at[pl.ds(0, 7)])
            for j in (1, 0):
                core = (c + j) % 2
                cols = pl.ds(pl.multiple_of(core * HALF + first, 128), width)
                result = dot(turned[...], wd[:, cols])
                ys[p][4 * j : 4 * j + 4] = result.astype(BF16).reshape(4, SLOTS, width)
                for k in (2, 1, 3, 0):
                    to = along(last, k)
                    src = ys[p].at[4 * j + to]
                    dst = yr[p].at[here[last] * 2 + c]
                    if k == 0 and j == 0:
                        local = pltpu.make_async_copy(src, dst, loc_sem.at[len(PARTS) + p])
                        local.start()
                        locals_out[p] = local
                    else:
                        stage[p].send(src, dst, device(**{last: to, "c": core}))
    for wave in BACK:
        for p in wave:
            order, first, width = PARTS[p]
            a, b, last = ORDER[order]
            stage[p].wait_recv()
            locals_out[p].wait()
            summed = lax.dot_general(
                comb[order], yr[p][...].reshape(8 * SLOTS, width), (((0,), (0,)), ((), ())),
                preferred_element_type=F32,
            )
            ps[p][...] = summed.astype(BF16).reshape(4, 64, width)
            stage[p] = Group(ps[p].at[pl.ds(0, 3)])
            for k in (2, 1, 3):
                to = along(b, k)
                stage[p].send(ps[p].at[to], rb[p].at[k], device(**{b: to}))
        for p in wave:
            order, first, width = PARTS[p]
            a, b, last = ORDER[order]
            stage[p].wait_recv()
            total = ps[p][here[b]].astype(F32)
            for k in (1, 2, 3):
                total = total + rb[p][k].astype(F32)
            ra_s[p][...] = total.astype(BF16).reshape(4, 16, width)
            stage[p] = Group(ra_s[p].at[pl.ds(0, 3)])
            for k in (2, 1, 3):
                to = along(a, k)
                stage[p].send(ra_s[p].at[to], ra_r[p].at[k], device(**{a: to}))
    for wave in BACK:
        for p in wave:
            order, first, width = PARTS[p]
            a, b, last = ORDER[order]
            stage[p].wait_recv()
            total = ra_s[p][here[a]].astype(F32)
            for k in (1, 2, 3):
                total = total + ra_r[p][k].astype(F32)
            cols = slice(first, first + width)
            hidden[:, cols] = hidden[:, cols] + total

    fin_s[1] = hidden[other_rows, :]
    fin = remote(fin_s.at[1], fin_r, sibling)
    out_ref[:, own_cols] = hidden[own_rows, :].astype(BF16)
    fin.wait_recv()
    out_ref[:, other_cols] = fin_r[...].astype(BF16)
    for group in groups:
        group.wait_send()


GROUPS = 11 + 6 * len(PARTS)


def shards(
    queries, new_keys, new_values, key_cache, value_cache, lengths, residual_in, query_gain, key_gain,
    out_proj, norm_gain, expert_ids, gate_weights, expert_gate, expert_up, expert_down,
):
    anywhere = pl.BlockSpec(memory_space=pl.ANY)

    def each(shape_of):
        return [VMEM(shape_of(width), BF16) for _, _, width in PARTS]

    return pl.pallas_call(
        kernel,
        out_shape=jax.ShapeDtypeStruct((8, D), BF16),
        in_specs=[anywhere] * 16,
        out_specs=pl.BlockSpec(memory_space=pltpu.VMEM),
        scratch_shapes=[
            VMEM((64, 32, 128), BF16), VMEM((64, 2, 128), BF16), VMEM((64, 2, 128), BF16),
            VMEM((64, 2, 32, 128), BF16), VMEM((64, 2, 32, 128), BF16), pltpu.SMEM((64,), jnp.int32),
            VMEM((8, D), BF16), VMEM((1, 128), F32), VMEM((1, 128), F32), VMEM((1, D), F32),
            VMEM((8, 8), jnp.int32), VMEM((8, 8), F32),
            VMEM((512, D), BF16), VMEM((D, FFW), BF16), VMEM((D, FFW), BF16), VMEM((FFW, D), BF16),
            VMEM((128, 512), BF16), VMEM((128, 512), BF16), VMEM((32, 16, 128), F32), VMEM((4, 32, 16, 128), BF16), VMEM((128, 128), F32),
            VMEM((128, 128), F32), VMEM((128, 128), F32), VMEM((8, 4, 4, 16, 128), BF16),
            VMEM((8, 8, 128), F32), VMEM((64, 512), BF16),
            VMEM((2, 64, 1024), BF16), VMEM((2, 64, 1024), BF16), VMEM((2, 64, 1024), BF16),
            VMEM((4, 2, 16, 1024), BF16), VMEM((16, HALF), F32),
            VMEM((16, 128), F32), VMEM((16, 128), F32),
            VMEM((8, 128), F32), VMEM((8, 8, 128), F32), VMEM((4, 4, 8, 128), F32),
            VMEM((4, 4, 4, 2, 8, 128), F32), VMEM((256, 128), F32),
            VMEM((3, 8 * SLOTS, 256), BF16), VMEM((3, 8 * SLOTS, 256), BF16),
            VMEM((384, D), BF16), VMEM((2, 384, 384), BF16), VMEM((2, 384, 384), BF16),
            VMEM((2, 384, FFW), F32), VMEM((384, FFW), BF16), VMEM((2, 384, FFW), BF16),
            each(lambda w: (4, 4, 16, w)),
            each(lambda w: (8, SLOTS, w)),
            each(lambda w: (2, 4, SLOTS, w)),
            each(lambda w: (8, SLOTS, w)),
            each(lambda w: (8, SLOTS, w)),
            each(lambda w: (4, 64, w)), each(lambda w: (4, 64, w)),
            each(lambda w: (4, 16, w)), each(lambda w: (4, 16, w)),
            VMEM((2, 8, HALF), F32), VMEM((8, HALF), F32),
            pltpu.SemaphoreType.DMA((12,)), pltpu.SemaphoreType.DMA((4,)), pltpu.SemaphoreType.DMA((2 * len(PARTS),)),
            pltpu.SemaphoreType.DMA((GROUPS,)), pltpu.SemaphoreType.DMA((GROUPS,)),
        ],
        compiler_params=pltpu.CompilerParams(
            collective_id=0, has_side_effects=True, vmem_limit_bytes=60 * 2**20
        ),
        cost_estimate=pl.CostEstimate(flops=10**10, bytes_accessed=26 * 2**20, transcendentals=10**6),
    )(
        queries, new_keys, new_values, key_cache, value_cache, lengths, residual_in,
        query_gain.reshape(1, 128), key_gain.reshape(1, 128), norm_gain.reshape(1, D),
        expert_ids, gate_weights, out_proj, expert_gate, expert_up, expert_down,
    )


def solution(mesh):
    rows = P(("dp", "tensor"), None)
    experts = P(("dp", "tensor"), None, None)
    cache = P("dp", None, "tensor", None)
    heads = P("dp", None, None)
    return jax.shard_map(
        shards,
        mesh=mesh,
        in_specs=(
            heads, heads, heads, cache, cache, P("dp"), rows, P(), P(),
            P("tensor", None), P(), rows, rows, experts, experts, experts,
        ),
        out_specs=rows,
        check_vma=False,
    )
```
